512 devices in a mesh: rep: 32 (over y, x_hi, core), shard: 16 (over z, x_lo).
Axes of the slice: x: 4 (x_hi: 2, x_lo: 2; x = x_hi * 2 + x_lo), y: 8, z: 8, core: 2. Of those that a mesh axis runs over, the one named last changes fastest.
Arguments:
- tokens: bfloat16 [65536, 8192], P(('rep', 'shard')), may hold values from -24 to 24
- key_grad: bfloat16 [65536, 512], P(('rep', 'shard')), may hold values from -150 to 150
- weight_codes: bfloat16 [8192, 512], P('shard'), may hold values from -0.0625 to 0.0625
- block_scales: float32 [64], P('shard'), may hold values from 0.5 to 2
Outputs:
- input_grad: bfloat16 [65536, 8192], P(('rep', 'shard'))
- weight_grad: float32 [8192, 512], P('shard')
- peak_values: float32 [2], replicated
The draws below stay inside these ranges and needn't reach their ends.
All inputs are finite; a program needn't handle non-finite values.
Results may differ from the reference program's by a relative error of at most 0.008.
Values may be sent and summed in bfloat16 or wider, within the bound.
No kernel may reach another device: no remote copies, remote signals or barrier semaphores. Data moves between devices by JAX's collectives and lax.ppermute only.
A program may use at most 64 MiB of HBM per device.

```python
import math
import jax
import jax.numpy as jnp
from jax import lax

D = 8192
HD = 128
KVH = 4
QBLOCK = 128
KW = 512
TOKENS = 65536
N_REP = 32


def draw_key_grad(key, part):
    key = jax.random.fold_in(key, 7)
    row_key, value_key = jax.random.split(key)
    positions = jnp.arange(TOKENS, dtype=jnp.float32)[:, None]
    growth = jnp.exp(math.log(3.0) * positions / TOKENS)
    spread = jnp.exp(jax.random.uniform(row_key, (TOKENS, 1), minval=0.0, maxval=math.log(10.0)))
    values = jnp.clip(jax.random.normal(value_key, (TOKENS, KVH * HD)), -5.0, 5.0)
    return (values * growth * spread).astype(jnp.bfloat16)


def spiked(values, key, source, target, shards_of, factor):
    def block_of(dim):
        return (jnp.arange(values.shape[dim]) // (values.shape[dim] // shards_of)).reshape((-1,) + (1,) * (values.ndim - 1 - dim))

    near = jax.random.permutation(key, shards_of)[block_of(target)]
    other_side = (block_of(target) + shards_of // 2) % shards_of
    return jnp.where((block_of(source) == near) | (block_of(source) == other_side), factor * values, values)


def block_levels(key, extent, shards, smallest, high):
    level = 1.0
    for position, shards_of in shards:
        draws = jax.random.uniform(jax.random.fold_in(jax.random.fold_in(key, 6), position), (shards_of,), jnp.float32, smallest / len(shards), high / len(shards))
        level = level * jnp.repeat(jnp.exp(draws), extent[position] // shards_of).reshape((-1,) + (1,) * (len(extent) - 1 - position))
    return level


def normal_values(rng, dims, width, bound, cuts=(), kind=jnp.bfloat16):
    drawn = jax.random.normal(rng, dims, jnp.float32) * width
    if len(cuts) > 0:
        drawn = block_levels(rng, dims, cuts, -0.22, 0.18) * drawn
    return jnp.clip(drawn, min=-bound, max=bound).astype(kind)


def bell_draw_with(stream_key, extent, scale, bound, cuts, heavy, held_as=jnp.bfloat16):
    entries = scale * jax.random.normal(stream_key, extent, jnp.float32)
    if cuts:
        entries = entries * block_levels(stream_key, extent, cuts, -0.22, 0.18)
    return jnp.clip(spiked(entries, jax.random.fold_in(stream_key, 3), *heavy), -bound, bound).astype(held_as)


def setup_inputs(seed: int = 0) -> dict:
    key_list = jax.random.split(jax.random.key(seed), 5)
    return {
        "tokens": bell_draw_with(key_list[0], (TOKENS, D), 1.0, 24.0, ((0, 512),), (0, 1, 512, 6.0)),
        "key_grad": draw_key_grad(jax.random.fold_in(key_list[4], 71), 0),
        "weight_codes": normal_values(key_list[2], (D, KW), D ** -0.5, 0.0625, ((0, 16),)),
        "block_scales": jnp.clip(jnp.exp(math.log(2.0) - 1.3862944 * jax.random.uniform(key_list[3], (D // QBLOCK,), jnp.float32) ** block_levels(key_list[3], (D // QBLOCK,), ((0, 16),), -0.2, 0.2)), 0.5, 2.0),
    }


def reference(tokens, key_grad, weight_codes, block_scales):
    scale_rows = jnp.repeat(block_scales, QBLOCK)
    weight = (weight_codes.astype(jnp.float32) * scale_rows[:, None]).astype(jnp.bfloat16)

    def project_block(grad_block):
        product = lax.dot_general(grad_block, weight, (((1,), (1,)), ((), ())), preferred_element_type=jnp.float32)
        return product.astype(jnp.bfloat16)
    grad_blocks = key_grad.reshape(N_REP, TOKENS // N_REP, KVH * HD)
    input_grad = lax.map(project_block, grad_blocks).reshape(TOKENS, D)
    factor = 1.0 / math.sqrt(TOKENS)
    weight_grad = lax.dot_general(tokens, key_grad, (((0,), (0,)), ((), ())), preferred_element_type=jnp.float32) * factor
    peak_values = jnp.stack([jnp.max(jnp.abs(input_grad.astype(jnp.float32))), jnp.max(jnp.abs(weight_grad))])
    return (input_grad, weight_grad, peak_values)
```

```python
import math

import jax
import jax.numpy as jnp
from jax import lax
from jax.sharding import Mesh
from jax.sharding import PartitionSpec as P

QBLOCK = 128
AXES = ("yh", "yl", "xh", "core", "zh", "zl", "xl")
SIZES = (4, 2, 2, 2, 4, 2, 2)
CUBE = ("yl", "core", "zl", "xl")
SPREAD = ("yh", "xh", "zh")
PLANE = ("yh", "yl", "xh")
BF16 = jnp.bfloat16
F32 = jnp.float32


def shard_swap():
    pairs = []
    for yl in range(2):
        for core in range(2):
            for zh in range(4):
                source = (yl * 2 + core) * 4 + zh
                target = zh * 4 + (yl * 2 + core)
                pairs.append((source, target))
    return pairs


def peak_rows(first, second):
    row = jnp.concatenate([jnp.full((256,), first, BF16), jnp.full((256,), second, BF16)])
    return jnp.broadcast_to(row[None], (16, 512))


def local(tokens, key_grad, weight_codes, block_scales):
    count, width = tokens.shape
    kw = key_grad.shape[1]
    factor = 1.0 / math.sqrt(512 * count)
    scale_rows = jnp.repeat(block_scales, QBLOCK)
    weight = (weight_codes.astype(F32) * scale_rows[:, None]).astype(BF16)
    weight = lax.ppermute(weight, ("yl", "core", "zh"), shard_swap())

    parts = tokens.reshape(count, 4, 4, 4, 128).transpose(3, 2, 0, 1, 4).reshape(16, count, 512)
    keys = jnp.broadcast_to(key_grad.reshape(1, 2, 1, count // 2, kw), (2, 2, 4, count // 2, kw))
    packed = jnp.concatenate([parts, keys.reshape(16, count // 2, kw)], axis=1)
    got = lax.all_to_all(packed, CUBE, 0, 0, tiled=True)
    cols = got[:, :count]
    halves = lax.all_gather(got[:, count:], "core", axis=1, tiled=True)

    share = lax.dot_general(cols, halves, (((0, 1), (0, 1)), ((), ())), preferred_element_type=F32)
    share = share.astype(BF16).reshape(4, 8, 16, kw).transpose(1, 0, 2, 3).reshape(32, 16, kw)
    terms = lax.all_to_all(share, SPREAD, 0, 0, tiled=True)
    piece = (jnp.sum(terms.astype(F32), axis=0) * factor).astype(BF16)
    weight_peak = jnp.max(jnp.abs(piece))

    back = lax.dot_general(halves, weight, (((2,), (1,)), ((), ())), preferred_element_type=F32)
    back = back.astype(BF16)
    input_peak = jnp.max(jnp.abs(back))
    rows = jnp.broadcast_to(peak_rows(input_peak, weight_peak)[None], (16, 16, 512))
    back = lax.all_to_all(jnp.concatenate([back, rows], axis=1), CUBE, 0, 0, tiled=True)
    input_grad = back[:, :count].transpose(1, 0, 2).reshape(count, width)
    peaks = jnp.max(back[:, count:].reshape(16, 16, 2, 256), axis=(0, 1, 3))

    sent = jnp.concatenate([piece, peak_rows(peaks[0], peaks[1])], axis=0)
    sent = jnp.broadcast_to(sent[None], (16,) + sent.shape)
    plane = lax.all_to_all(sent, PLANE, 0, 0, tiled=True)
    peaks = jnp.max(plane[:, 16:].reshape(16, 16, 2, 256), axis=(0, 1, 3)).astype(F32)
    both = lax.all_gather(plane[:, :16], "core", axis=0, tiled=False)
    both = both.reshape(2, 4, 2, 2, 16, kw).transpose(2, 0, 1, 3, 4, 5)
    weight_grad = both.reshape(512, kw).astype(F32)
    tile = jnp.broadcast_to(peaks[None, :, None], (4, 2, 128))
    peaks = jnp.max(lax.all_to_all(tile, "zh", 0, 0, tiled=True), axis=(0, 2))
    return (input_grad, weight_grad, peaks)


def solution(mesh):
    fine = Mesh(mesh.devices.reshape(SIZES), AXES)
    shard = ("zh", "zl", "xl")
    return jax.shard_map(
        local,
        mesh=fine,
        in_specs=(P(AXES, None), P(AXES, None), P(shard, None), P(shard)),
        out_specs=(P(AXES, None), P(shard, None), P()),
        check_vma=False,
    )
```

```python
import math

import jax
import jax.numpy as jnp
from jax import lax
from jax.experimental import pallas as pl
from jax.experimental.pallas import tpu as pltpu
from jax.sharding import Mesh
from jax.sharding import PartitionSpec as P

QBLOCK = 128
AXES = ("yh", "yl", "xh", "core", "zh", "zl", "xl")
SIZES = (4, 2, 2, 2, 4, 2, 2)
CUBE = ("yl", "core", "zl", "xl")
SPREAD = ("yh", "xh", "zh")
PLANE = ("yh", "yl", "xh")
BF16 = jnp.bfloat16
F32 = jnp.float32
COUNT = 128
HALF = COUNT // 2
KW = 512
PACK = COUNT + HALF
RETURN = COUNT + 16
PARAMS = pltpu.CompilerParams(vmem_limit_bytes=24 * 2**20)


def cost(flops, moved):
    return pl.CostEstimate(flops=flops, bytes_accessed=moved, transcendentals=0)


def shard_swap():
    pairs = []
    for yl in range(2):
        for core in range(2):
            for zh in range(4):
                source = (yl * 2 + core) * 4 + zh
                target = zh * 4 + (yl * 2 + core)
                pairs.append((source, target))
    return pairs


def pack_kernel(tokens, keys, out):
    for part in range(16):
        q, e = part // 4, part % 4
        first = (q % 2) * HALF
        second = HALF - first
        lanes = pl.ds(e * 512 + q * 128, 128)
        out[part, 0:HALF, :] = tokens[first : first + HALF, lanes]
        out[part, HALF:COUNT, :] = tokens[second : second + HALF, lanes]
        out[part, COUNT:PACK, :] = keys[first : first + HALF, :]


def pack(tokens, key_grad):
    return pl.pallas_call(
        pack_kernel,
        grid=(4,),
        in_specs=[
            pl.BlockSpec((COUNT, 2048), lambda i: (0, i)),
            pl.BlockSpec((COUNT, 128), lambda i: (0, i)),
        ],
        out_specs=pl.BlockSpec((16, PACK, 128), lambda i: (0, 0, i)),
        out_shape=jax.ShapeDtypeStruct((16, PACK, KW), BF16),
        compiler_params=PARAMS,
        cost_estimate=cost(0, 5 * 2**20),
        name="pack",
    )(tokens, key_grad)


def share_kernel(got, other, out, acc):
    step = pl.program_id(0)

    @pl.when(step == 0)
    def _():
        acc[...] = jnp.zeros_like(acc)

    total = acc[...]
    for rows, keys in ((got[:, 0:HALF, :], got[:, COUNT:PACK, :]), (got[:, HALF:COUNT, :], other[...])):
        total += lax.dot_general(
            rows.reshape(-1, KW),
            keys.reshape(-1, KW),
            (((0,), (0,)), ((), ())),
            preferred_element_type=F32,
        )
    acc[...] = total

    @pl.when(step == pl.num_programs(0) - 1)
    def _():
        for zh in range(4):
            for w in range(8):
                row = (zh * 8 + w) * 16
                out[w * 4 + zh] = acc[row : row + 16, :].astype(BF16)


def share_of(got, other):
    return pl.pallas_call(
        share_kernel,
        grid=(4,),
        in_specs=[
            pl.BlockSpec((4, PACK, KW), lambda i: (i, 0, 0)),
            pl.BlockSpec((4, HALF, KW), lambda i: (i, 0, 0)),
        ],
        out_specs=pl.BlockSpec((32, 16, KW), lambda i: (0, 0, 0)),
        out_shape=jax.ShapeDtypeStruct((32, 16, KW), BF16),
        scratch_shapes=[pltpu.VMEM((KW, KW), F32)],
        compiler_params=PARAMS,
        cost_estimate=cost(2**30, 5 * 2**20),
        name="share",
    )(got, other)


def product_kernel(mine, other, weight, out, peak):
    step = pl.program_id(0)

    @pl.when(step == 0)
    def _():
        peak[...] = jnp.zeros_like(peak)

    high = peak[...]
    for half, keys in enumerate((mine, other)):
        product = lax.dot_general(
            keys[...].reshape(-1, KW), weight[...], (((1,), (1,)), ((), ())), preferred_element_type=F32
        )
        rounded = product.astype(BF16)
        out[:, half * HALF : (half + 1) * HALF, :] = rounded.reshape(4, HALF, KW)
        size = jnp.abs(rounded.astype(F32)).reshape(-1, 8, KW)
        high = jnp.maximum(high, jnp.max(size, axis=0))
    peak[...] = high
    out[:, COUNT:RETURN, :] = jnp.zeros((4, RETURN - COUNT, KW), BF16)


def product_of(got, other, weight):
    return pl.pallas_call(
        product_kernel,
        grid=(4,),
        in_specs=[
            pl.BlockSpec((4, HALF, KW), lambda i: (i, 2, 0)),
            pl.BlockSpec((4, HALF, KW), lambda i: (i, 0, 0)),
            pl.BlockSpec((KW, KW), lambda i: (0, 0)),
        ],
        out_specs=[
            pl.BlockSpec((4, RETURN, KW), lambda i: (i, 0, 0)),
            pl.BlockSpec((8, KW), lambda i: (0, 0)),
        ],
        out_shape=[
            jax.ShapeDtypeStruct((16, RETURN, KW), BF16),
            jax.ShapeDtypeStruct((8, KW), F32),
        ],
        compiler_params=PARAMS,
        cost_estimate=cost(2**30, 5 * 2**20),
        name="product",
    )(got, other, weight)


def reduce_kernel(factor, terms, high, back_in, piece, back, rows, sem):
    total = terms[0].astype(F32)
    for k in range(1, 32):
        total += terms[k].astype(F32)
    rounded = (total * factor).astype(BF16)
    piece[...] = rounded
    first = jnp.max(high[...])
    second = jnp.max(jnp.abs(rounded.astype(F32)))
    lane = lax.broadcasted_iota(jnp.int32, (16, KW), 1)
    line = jnp.where(lane < 256, first, second).astype(BF16)
    for k in range(16):
        rows[k] = line
    copy = pltpu.make_async_copy(rows, back.at[:, COUNT:RETURN, :], sem)
    copy.start()
    copy.wait()


def reduce_terms(factor, terms, high, back):
    vmem = pl.BlockSpec(memory_space=pltpu.VMEM)
    return pl.pallas_call(
        lambda *refs: reduce_kernel(factor, *refs),
        in_specs=[vmem, vmem, pl.BlockSpec(memory_space=pl.ANY)],
        out_specs=[vmem, pl.BlockSpec(memory_space=pl.ANY)],
        out_shape=[
            jax.ShapeDtypeStruct((16, KW), BF16),
            jax.ShapeDtypeStruct(back.shape, BF16),
        ],
        input_output_aliases={2: 1},
        scratch_shapes=[pltpu.VMEM((16, 16, KW), BF16), pltpu.SemaphoreType.DMA],
        compiler_params=PARAMS,
        cost_estimate=cost(2**18, 2**20),
        name="reduce_terms",
    )(terms, high, back)


def spread_kernel(rows, piece, out):
    high = jnp.max(rows[...].astype(F32), axis=0)
    lane = lax.broadcasted_iota(jnp.int32, (16, KW), 1)
    first = jnp.max(jnp.where(lane < 256, high, 0.0))
    second = jnp.max(jnp.where(lane < 256, 0.0, high))
    line = jnp.where(lane < 256, first, second).astype(BF16)
    for k in range(16):
        out[k, 0:16, :] = piece[...]
        out[k, 16:32, :] = line


def spread(back, piece):
    return pl.pallas_call(
        spread_kernel,
        grid=(1,),
        in_specs=[
            pl.BlockSpec((16, 16, KW), lambda i: (0, COUNT // 16, 0)),
            pl.BlockSpec((16, KW), lambda i: (0, 0)),
        ],
        out_specs=pl.BlockSpec((16, 32, KW), lambda i: (0, 0, 0)),
        out_shape=jax.ShapeDtypeStruct((16, 32, KW), BF16),
        compiler_params=PARAMS,
        cost_estimate=cost(2**17, 2**20),
        name="spread",
    )(back, piece)


def unpack_kernel(back, out):
    second = pl.program_id(0) % 2

    def put(first):
        for e in range(4):
            lanes = pl.ds(e * 512, 512)
            out[first : first + HALF, lanes] = back[e, 0:HALF, :]
            out[HALF - first : COUNT - first, lanes] = back[e, HALF:COUNT, :]

    @pl.when(second == 0)
    def _():
        put(0)

    @pl.when(second == 1)
    def _():
        put(HALF)


def unpack(back):
    return pl.pallas_call(
        unpack_kernel,
        grid=(4,),
        in_specs=[pl.BlockSpec((4, RETURN, KW), lambda i: (i, 0, 0))],
        out_specs=pl.BlockSpec((COUNT, 2048), lambda i: (0, i)),
        out_shape=jax.ShapeDtypeStruct((COUNT, 8192), BF16),
        compiler_params=PARAMS,
        cost_estimate=cost(0, 5 * 2**20),
        name="unpack",
    )(back)


def merge_kernel(mine, other, out):
    core = lax.axis_index("core")
    for yl in range(2):
        for source, at in ((mine, core), (other, 1 - core)):
            for yh in range(4):
                for xh in range(2):
                    row = pl.multiple_of(yl * 256 + at * 128 + (yh * 2 + xh) * 16, 16)
                    out[pl.ds(row, 16), :] = source[(yh * 2 + yl) * 2 + xh, 0:16, :].astype(F32)


def merge(plane, other):
    vmem = pl.BlockSpec(memory_space=pltpu.VMEM)
    return pl.pallas_call(
        merge_kernel,
        in_specs=[vmem, vmem],
        out_specs=vmem,
        out_shape=jax.ShapeDtypeStruct((512, KW), F32),
        compiler_params=PARAMS,
        cost_estimate=cost(0, 2 * 2**20),
        name="merge",
    )(plane, other)


def local(tokens, key_grad, weight_codes, block_scales):
    factor = 1.0 / math.sqrt(512 * COUNT)
    scale_rows = jnp.repeat(block_scales, QBLOCK)
    weight = (weight_codes.astype(F32) * scale_rows[:, None]).astype(BF16)
    weight = lax.ppermute(weight, ("yl", "core", "zh"), shard_swap())

    got = lax.all_to_all(pack(tokens, key_grad), CUBE, 0, 0, tiled=True)
    got, weight = lax.optimization_barrier((got, weight))
    other = lax.ppermute(got[:, COUNT:], "core", [(0, 1), (1, 0)])

    terms = lax.all_to_all(share_of(got, other), SPREAD, 0, 0, tiled=True)

    back, high = product_of(got, other, weight)
    piece, back = reduce_terms(factor, terms, high, back)
    back = lax.all_to_all(back, CUBE, 0, 0, tiled=True)
    input_grad = unpack(back)

    plane = lax.all_to_all(spread(back, piece), PLANE, 0, 0, tiled=True)
    peaks = jnp.max(plane[:, 16:].reshape(16, 16, 2, 256), axis=(0, 1, 3)).astype(F32)
    other = lax.ppermute(plane[:, :16], "core", [(0, 1), (1, 0)])
    weight_grad = merge(plane, other)
    tile = jnp.broadcast_to(peaks[None, :, None], (4, 2, 128))
    peaks = jnp.max(lax.all_to_all(tile, "zh", 0, 0, tiled=True), axis=(0, 2))
    return (input_grad, weight_grad, peaks)


def solution(mesh):
    fine = Mesh(mesh.devices.reshape(SIZES), AXES)
    shard = ("zh", "zl", "xl")
    return jax.shard_map(
        local,
        mesh=fine,
        in_specs=(P(AXES, None), P(AXES, None), P(shard, None), P(shard)),
        out_specs=(P(AXES, None), P(shard, None), P()),
        check_vma=False,
    )
```

```python
import math

import jax
import jax.numpy as jnp
from jax import lax
from jax.experimental import pallas as pl
from jax.experimental.pallas import tpu as pltpu
from jax.sharding import Mesh
from jax.sharding import PartitionSpec as P

QBLOCK = 128
AXES = ("yh", "yl", "xh", "core", "z", "xl")
SIZES = (4, 2, 2, 2, 8, 2)
GROUP = ("yl", "xh", "core", "xl")
SPREAD = ("yh", "z")
PLANE = ("yh", "yl", "xh")
SHIFT = (0, 4, 1, 7, 2, 6, 3, 5)
BF16 = jnp.bfloat16
F32 = jnp.float32
COUNT = 128
HALF = COUNT // 2
KW = 512
PACK = COUNT + HALF
RETURN = COUNT + 16
WIDE = KW + 128
PARAMS = pltpu.CompilerParams(vmem_limit_bytes=24 * 2**20)
VMEM = pl.BlockSpec(memory_space=pltpu.VMEM)
ANY = pl.BlockSpec(memory_space=pl.ANY)


def call(kernel, name, out_shape, in_specs, out_specs, flops, moved, **more):
    return pl.pallas_call(
        kernel,
        in_specs=in_specs,
        out_specs=out_specs,
        out_shape=out_shape,
        compiler_params=PARAMS,
        cost_estimate=pl.CostEstimate(flops=flops, bytes_accessed=moved, transcendentals=0),
        name=name,
        **more,
    )


def array(shape, dtype=BF16):
    return jax.ShapeDtypeStruct(shape, dtype)


def pack_kernel(tokens, keys, codes, scales, out, weight, columns, own, held, sems):
    loads = [
        pltpu.make_async_copy(tokens.at[:, pl.ds(m * 2048, 2048)], columns.at[m], sems.at[m]) for m in range(4)
    ]
    loads.append(pltpu.make_async_copy(keys, own, sems.at[4]))
    loads.append(pltpu.make_async_copy(codes, held, sems.at[5]))
    for load in loads:
        load.start()
    low = lax.broadcasted_iota(jnp.int32, (HALF, 128), 1) < 64
    for m in range(4):
        loads[m].wait()
        for t in range(4):
            for e in range(2):
                for half in range(2):
                    rows = pl.ds(half * HALF, HALF)
                    even = columns[m, rows, pl.ds(e * 512 + t * 128, 128)]
                    odd = columns[m, rows, pl.ds(1024 + e * 512 + t * 128, 128)]
                    for core in range(2):
                        first, second = (even, odd) if core == 0 else (odd, even)
                        at = HALF * (half ^ core)
                        out[t * 4 + core * 2 + e, at : at + HALF, m * 128 : (m + 1) * 128] = jnp.where(
                            low, first, second
                        )
    loads[4].wait()
    for part in range(16):
        core = part // 2 % 2
        out[part, COUNT:PACK, :] = own[core * HALF : (core + 1) * HALF, :]
    loads[5].wait()
    for block in range(4):
        rows = pl.ds(block * QBLOCK, QBLOCK)
        weight[rows, :] = (held[rows, :].astype(F32) * scales[block]).astype(BF16)


def pack(tokens, key_grad, codes, scales):
    return call(
        pack_kernel,
        "pack",
        [array((16, PACK, KW)), array((512, KW))],
        [ANY, ANY, ANY, pl.BlockSpec(memory_space=pltpu.SMEM)],
        [VMEM, VMEM],
        0,
        6 * 2**20,
        scratch_shapes=[
            pltpu.VMEM((4, COUNT, 2048), BF16),
            pltpu.VMEM((COUNT, KW), BF16),
            pltpu.VMEM((512, KW), BF16),
            pltpu.SemaphoreType.DMA((6,)),
        ],
    )(tokens, key_grad, codes, scales)


def gradients(rows, keys):
    return lax.dot_general(
        rows.reshape(-1, KW), keys.reshape(-1, KW), (((0,), (0,)), ((), ())), preferred_element_type=F32
    )


def products(keys, weight):
    out = lax.dot_general(
        keys.reshape(-1, KW), weight, (((1,), (1,)), ((), ())), preferred_element_type=F32
    ).astype(BF16)
    return out, jnp.max(jnp.abs(out.astype(F32)).reshape(-1, 8, KW), axis=0)


def own_kernel(got, weight, total, product, high):
    total[...] = gradients(got[:, 0:HALF, :], got[:, COUNT:PACK, :])
    out, size = products(got[:, COUNT:PACK, :], weight[...])
    product[...] = out.reshape(16, HALF, KW)
    high[...] = size


def own_half(got, weight):
    return call(
        own_kernel,
        "own_half",
        [array((KW, KW), F32), array((16, HALF, KW)), array((8, KW), F32)],
        [VMEM] * 2,
        [VMEM] * 3,
        2**30,
        5 * 2**20,
    )(got, weight)


def other_kernel(got, other, weight, total, product, high_in, share, back, high):
    core = lax.axis_index("core")
    out, size = products(other[...], weight[...])
    back[:, 0:HALF, :] = product[...]
    back[:, HALF:COUNT, :] = out.reshape(16, HALF, KW)
    back[:, COUNT:RETURN, :] = jnp.zeros((16, RETURN - COUNT, KW), BF16)
    high[...] = jnp.maximum(high_in[...], size)
    summed = (total[...] + gradients(got[:, HALF:COUNT, :], other[...])).astype(BF16)
    for m in range(4):
        for s in range(2):
            z = 2 * m + jnp.where(core == 0, s, 1 - s)
            for yh in range(4):
                row = m * 128 + s * 64 + yh * 16
                share[yh * 8 + z] = summed[row : row + 16, :]


def other_half(got, other, weight, total, product, high):
    return call(
        other_kernel,
        "other_half",
        [array((32, 16, KW)), array((16, RETURN, KW)), array((8, KW), F32)],
        [VMEM] * 6,
        [VMEM] * 3,
        2**30,
        7 * 2**20,
    )(got, other, weight, total, product, high)


def reduce_kernel(factor, terms, high, back_in, piece, back, rows, sem):
    total = terms[0].astype(F32)
    for k in range(1, 32):
        total += terms[k].astype(F32)
    rounded = (total * factor).astype(BF16)
    piece[...] = rounded
    first = jnp.max(high[...])
    second = jnp.max(jnp.abs(rounded.astype(F32)))
    lane = lax.broadcasted_iota(jnp.int32, (16, KW), 1)
    line = jnp.where(lane < 256, first, second).astype(BF16)
    for k in range(16):
        rows[k] = line
    copy = pltpu.make_async_copy(rows, back.at[:, COUNT:RETURN, :], sem)
    copy.start()
    copy.wait()


def reduce_terms(factor, terms, high, back):
    return call(
        lambda *refs: reduce_kernel(factor, *refs),
        "reduce_terms",
        [array((16, KW)), array(back.shape)],
        [VMEM, VMEM, ANY],
        [VMEM, ANY],
        2**18,
        2**20,
        input_output_aliases={2: 1},
        scratch_shapes=[pltpu.VMEM((16, 16, KW), BF16), pltpu.SemaphoreType.DMA],
    )(terms, high, back)


def spread_kernel(rows, piece, out):
    high = jnp.max(rows[...].astype(F32), axis=0)
    lane = lax.broadcasted_iota(jnp.int32, (16, KW), 1)
    first = jnp.max(jnp.where(lane < 256, high, 0.0))
    second = jnp.max(jnp.where(lane < 256, 0.0, high))
    lane = lax.broadcasted_iota(jnp.int32, (16, 128), 1)
    line = jnp.where(lane < 64, first, second).astype(BF16)
    for k in range(16):
        out[k, :, 0:KW] = piece[...]
        out[k, :, KW:WIDE] = line


def spread(back, piece):
    return call(
        spread_kernel,
        "spread",
        array((16, 16, WIDE)),
        [
            pl.BlockSpec((16, 16, KW), lambda i: (0, COUNT // 16, 0)),
            pl.BlockSpec((16, KW), lambda i: (0, 0)),
        ],
        pl.BlockSpec((16, 16, WIDE), lambda i: (0, 0, 0)),
        2**17,
        2**20,
        grid=(1,),
    )(back, piece)


def unpack_kernel(place, back, out):
    second = pl.program_id(0) % 2

    def put(first):
        for e in range(2):
            lanes = pl.ds(e * 512, 512)
            out[first : first + HALF, lanes] = back[e, 0:HALF, :]
            out[HALF - first : COUNT - first, lanes] = back[e, HALF:COUNT, :]

    @pl.when(second == 0)
    def _():
        put(0)

    @pl.when(second == 1)
    def _():
        put(HALF)


def unpack(place, back):
    return pl.pallas_call(
        unpack_kernel,
        grid_spec=pltpu.PrefetchScalarGridSpec(
            num_scalar_prefetch=1,
            grid=(8,),
            in_specs=[pl.BlockSpec((2, RETURN, KW), lambda i, place: (i, 0, 0))],
            out_specs=pl.BlockSpec((COUNT, 1024), lambda i, place: (0, place[i])),
        ),
        out_shape=array((COUNT, 8192)),
        compiler_params=PARAMS,
        cost_estimate=pl.CostEstimate(flops=0, bytes_accessed=5 * 2**20, transcendentals=0),
        name="unpack",
    )(place, back)


def tile_kernel(plane, out):
    high = jnp.max(plane[:, :, KW:WIDE].astype(F32), axis=0)
    high = jnp.max(high.reshape(2, 8, 128), axis=0)
    for k in range(8):
        out[k] = high


def tile_of(plane):
    return call(tile_kernel, "tile", array((8, 8, 128), F32), [VMEM], VMEM, 2**15, 2**17)(plane)


def merge_kernel(mine, other, out):
    turn = lax.rem(lax.axis_index("core") + lax.axis_index("z"), 2)
    for source, s in ((mine, turn), (other, 1 - turn)):
        for yh in range(4):
            for t in range(4):
                row = pl.multiple_of(t * 128 + s * 64 + yh * 16, 16)
                out[pl.ds(row, 16), :] = source[yh * 4 + t, :, 0:KW].astype(F32)


def merge(plane, other):
    return call(merge_kernel, "merge", array((512, KW), F32), [VMEM] * 2, VMEM, 0, 2 * 2**20)(plane, other)


def swap(x):
    return lax.ppermute(x, "core", [(0, 1), (1, 0)])


def shift_weight(weight):
    pairs = [(q * 8 + (z + SHIFT[q]) % 8, q * 8 + z) for q in range(8) for z in range(8)]
    return lax.ppermute(weight, ("yl", "xh", "core", "z"), pairs)


def local(tokens, key_grad, weight_codes, block_scales):
    factor = 1.0 / math.sqrt(512 * COUNT)
    place = lax.rem(jnp.array(SHIFT, jnp.int32) + lax.axis_index("z"), 8)

    packed, weight = pack(tokens, key_grad, weight_codes, block_scales)
    weight = shift_weight(weight)
    got = lax.all_to_all(packed, GROUP, 0, 0, tiled=True)
    other = swap(got[:, COUNT:])
    total, product, high = own_half(got, weight)
    share, back, high = other_half(got, other, weight, total, product, high)

    terms = lax.all_to_all(share, SPREAD, 0, 0, tiled=True)
    piece, back = reduce_terms(factor, terms, high, back)

    back = lax.all_to_all(back, GROUP, 0, 0, tiled=True)
    input_grad = unpack(place, back)

    plane = lax.all_to_all(spread(back, piece), PLANE, 0, 0, tiled=True)
    weight_grad = merge(plane, swap(plane))
    tile = lax.all_to_all(tile_of(plane), "z", 0, 0, tiled=True)
    tile, weight_grad, input_grad = lax.optimization_barrier((tile, weight_grad, input_grad))
    peaks = jnp.max(tile.reshape(64, 2, 64), axis=(0, 2))
    return (input_grad, weight_grad, peaks)


def solution(mesh):
    fine = Mesh(mesh.devices.reshape(SIZES), AXES)
    return jax.shard_map(
        local,
        mesh=fine,
        in_specs=(P(AXES, None), P(AXES, None), P(("z", "xl"), None), P(("z", "xl"))),
        out_specs=(P(AXES, None), P(("z", "xl"), None), P()),
        check_vma=False,
    )
```

```python
import math

import jax
import jax.numpy as jnp
from jax import lax
from jax.experimental import pallas as pl
from jax.experimental.pallas import tpu as pltpu
from jax.sharding import Mesh
from jax.sharding import PartitionSpec as P

QBLOCK = 128
AXES = ("yh", "yl", "xh", "core", "z", "xl")
SIZES = (4, 2, 2, 2, 8, 2)
GROUP = ("yl", "xh", "core", "xl")
SPREAD = ("yh", "z")
PLANE = ("yh", "yl", "xh")
SHIFT = (0, 4, 1, 7, 2, 6, 3, 5)
BF16 = jnp.bfloat16
F32 = jnp.float32
COUNT = 128
HALF = COUNT // 2
KW = 512
PACK = COUNT + HALF
WIDE = KW + 128
PARAMS = pltpu.CompilerParams(vmem_limit_bytes=24 * 2**20)
VMEM = pl.BlockSpec(memory_space=pltpu.VMEM)
ANY = pl.BlockSpec(memory_space=pl.ANY)


def call(kernel, name, out_shape, in_specs, out_specs, flops, moved, **more):
    return pl.pallas_call(
        kernel,
        in_specs=in_specs,
        out_specs=out_specs,
        out_shape=out_shape,
        compiler_params=PARAMS,
        cost_estimate=pl.CostEstimate(flops=flops, bytes_accessed=moved, transcendentals=0),
        name=name,
        **more,
    )


def array(shape, dtype=BF16):
    return jax.ShapeDtypeStruct(shape, dtype)


def pack_kernel(tokens, keys, codes, scales, out, weight, columns, own, held, ready, scaled, sems):
    loads = [
        pltpu.make_async_copy(tokens.at[:, pl.ds(z * 1024, 1024)], columns.at[z], sems.at[z]) for z in range(8)
    ]
    loads.append(pltpu.make_async_copy(keys, own, sems.at[8]))
    loads.append(pltpu.make_async_copy(codes, held, sems.at[9]))
    for load in loads[8:] + loads[:8]:
        load.start()
    stores = []
    loads[9].wait()
    for block in range(4):
        rows = pl.ds(block * QBLOCK, QBLOCK)
        scaled[rows, :] = (held[rows, :].astype(F32) * scales[block]).astype(BF16)
    stores.append(pltpu.make_async_copy(scaled, weight, sems.at[10]))
    stores[-1].start()
    loads[8].wait()
    for part in range(16):
        core = part // 2 % 2
        ready[part, COUNT:PACK, :] = own[core * HALF : (core + 1) * HALF, :]
    low = lax.broadcasted_iota(jnp.int32, (HALF, 128), 1) < 64
    for m in range(4):
        loads[2 * m].wait()
        loads[2 * m + 1].wait()
        lanes = pl.ds(m * 128, 128)
        for t in range(4):
            for e in range(2):
                for half in range(2):
                    rows = pl.ds(half * HALF, HALF)
                    column = pl.ds(e * 512 + t * 128, 128)
                    even = columns[2 * m, rows, column]
                    odd = columns[2 * m + 1, rows, column]
                    for core in range(2):
                        first, second = (even, odd) if core == 0 else (odd, even)
                        at = HALF * (half ^ core)
                        ready[t * 4 + core * 2 + e, at : at + HALF, lanes] = jnp.where(low, first, second)
        stores.append(pltpu.make_async_copy(ready.at[:, :, lanes], out.at[:, :, lanes], sems.at[11 + m]))
        stores[-1].start()
    for store in stores:
        store.wait()


def hbm(x):
    return pltpu.with_memory_space_constraint(x, pltpu.HBM)


def pack(tokens, key_grad, codes, scales):
    return call(
        pack_kernel,
        "pack",
        [pltpu.HBM((16, PACK, KW), BF16), pltpu.HBM((512, KW), BF16)],
        [ANY, ANY, ANY, pl.BlockSpec(memory_space=pltpu.SMEM)],
        [ANY, ANY],
        0,
        9 * 2**20,
        scratch_shapes=[
            pltpu.VMEM((8, COUNT, 1024), BF16),
            pltpu.VMEM((COUNT, KW), BF16),
            pltpu.VMEM((512, KW), BF16),
            pltpu.VMEM((16, PACK, KW), BF16),
            pltpu.VMEM((512, KW), BF16),
            pltpu.SemaphoreType.DMA((15,)),
        ],
    )(hbm(tokens), hbm(key_grad), hbm(codes), scales)


def gradients(rows, keys):
    return lax.dot_general(
        rows.reshape(-1, KW), keys.reshape(-1, KW), (((0,), (0,)), ((), ())), preferred_element_type=F32
    )


def products(keys, weight):
    out = lax.dot_general(
        keys.reshape(-1, KW), weight, (((1,), (1,)), ((), ())), preferred_element_type=F32
    ).astype(BF16)
    return out, jnp.max(jnp.abs(out.astype(F32)).reshape(-1, 8, KW), axis=0)


def own_kernel(got, weight, total, product, high):
    total[...] = gradients(got[:, 0:HALF, :], got[:, COUNT:PACK, :])
    out, size = products(got[:, COUNT:PACK, :], weight[...])
    product[...] = out.reshape(16, HALF, KW)
    high[...] = size


def own_half(got, weight):
    return call(
        own_kernel,
        "own_half",
        [array((KW, KW), F32), array((16, HALF, KW)), array((8, KW), F32)],
        [VMEM] * 2,
        [VMEM] * 3,
        2**30,
        5 * 2**20,
    )(got, weight)


def other_kernel(got, other, weight, total, product, high_in, share, back, high):
    core = lax.axis_index("core")
    out, size = products(other[...], weight[...])
    back[:, 0:HALF, :] = product[...]
    back[:, HALF:COUNT, :] = out.reshape(16, HALF, KW)
    high[...] = jnp.maximum(high_in[...], size)
    summed = (total[...] + gradients(got[:, HALF:COUNT, :], other[...])).astype(BF16)
    for m in range(4):
        for s in range(2):
            z = 2 * m + jnp.where(core == 0, s, 1 - s)
            for yh in range(4):
                row = m * 128 + s * 64 + yh * 16
                share[yh * 8 + z] = summed[row : row + 16, :]


def other_half(got, other, weight, total, product, high):
    return call(
        other_kernel,
        "other_half",
        [array((32, 16, KW)), array((16, COUNT, KW)), array((8, KW), F32)],
        [VMEM] * 6,
        [VMEM] * 3,
        2**30,
        7 * 2**20,
    )(got, other, weight, total, product, high)


def reduce_kernel(factor, terms, high, piece, peaks):
    total = terms[0].astype(F32)
    for k in range(1, 32):
        total += terms[k].astype(F32)
    rounded = (total * factor).astype(BF16)
    piece[...] = rounded
    first = jnp.max(high[...])
    second = jnp.max(jnp.abs(rounded.astype(F32)))
    lane = lax.broadcasted_iota(jnp.int32, (8, 128), 1)
    peaks[...] = jnp.where(lane < 64, first, second)


def reduce_terms(factor, terms, high):
    return call(
        lambda *refs: reduce_kernel(factor, *refs),
        "reduce_terms",
        [array((16, KW)), array((8, 128), F32)],
        [VMEM] * 2,
        [VMEM] * 2,
        2**18,
        2**20,
    )(terms, high)


def spread_kernel(piece, peaks, out):
    line = jnp.concatenate([peaks[...], peaks[...]], axis=0).astype(BF16)
    for k in range(16):
        out[k, :, 0:KW] = piece[...]
        out[k, :, KW:WIDE] = line


def spread(piece, peaks):
    return call(spread_kernel, "spread", array((16, 16, WIDE)), [VMEM] * 2, VMEM, 0, 2**19)(piece, peaks)


def unpack_kernel(place, back, out):
    second = pl.program_id(0) % 2

    def put(first):
        for e in range(2):
            lanes = pl.ds(e * 512, 512)
            out[first : first + HALF, lanes] = back[e, 0:HALF, :]
            out[HALF - first : COUNT - first, lanes] = back[e, HALF:COUNT, :]

    @pl.when(second == 0)
    def _():
        put(0)

    @pl.when(second == 1)
    def _():
        put(HALF)


def unpack(place, back):
    return pl.pallas_call(
        unpack_kernel,
        grid_spec=pltpu.PrefetchScalarGridSpec(
            num_scalar_prefetch=1,
            grid=(8,),
            in_specs=[pl.BlockSpec((2, COUNT, KW), lambda i, place: (i, 0, 0))],
            out_specs=pl.BlockSpec((COUNT, 1024), lambda i, place: (0, place[i])),
        ),
        out_shape=array((COUNT, 8192)),
        compiler_params=PARAMS,
        cost_estimate=pl.CostEstimate(flops=0, bytes_accessed=5 * 2**20, transcendentals=0),
        name="unpack",
    )(place, back)


def merge_kernel(mine, other, out, peaks):
    turn = lax.rem(lax.axis_index("core") + lax.axis_index("z"), 2)
    for source, s in ((mine, turn), (other, 1 - turn)):
        for yh in range(4):
            for t in range(4):
                row = pl.multiple_of(t * 128 + s * 64 + yh * 16, 16)
                out[pl.ds(row, 16), :] = source[yh * 4 + t, :, 0:KW].astype(F32)
    high = jnp.maximum(mine[:, :, KW:WIDE], other[:, :, KW:WIDE]).astype(F32)
    high = jnp.max(high.reshape(32, 8, 128), axis=0)
    low = lax.broadcasted_iota(jnp.int32, (8, 128), 1) < 64
    peaks[0] = jnp.max(jnp.where(low, high, 0.0))
    peaks[1] = jnp.max(jnp.where(low, 0.0, high))


def merge(plane, other):
    return call(
        merge_kernel,
        "merge",
        [array((512, KW), F32), array((2,), F32)],
        [VMEM] * 2,
        [VMEM, pl.BlockSpec(memory_space=pltpu.SMEM)],
        0,
        2 * 2**20,
    )(plane, other)


def over_shards(peaks):
    for step in (1, 2, 4):
        peaks = jnp.maximum(peaks, lax.ppermute(peaks, "z", [(z, (z + step) % 8) for z in range(8)]))
    return jnp.maximum(peaks, lax.ppermute(peaks, "xl", [(0, 1), (1, 0)]))


def swap(x):
    return lax.ppermute(x, "core", [(0, 1), (1, 0)])


def shift_weight(weight):
    pairs = [(q * 8 + (z + SHIFT[q]) % 8, q * 8 + z) for q in range(8) for z in range(8)]
    return lax.ppermute(weight, ("yl", "xh", "core", "z"), pairs)


def local(tokens, key_grad, weight_codes, block_scales):
    factor = 1.0 / math.sqrt(512 * COUNT)
    place = lax.rem(jnp.array(SHIFT, jnp.int32) + lax.axis_index("z"), 8)

    packed, weight = pack(tokens, key_grad, weight_codes, block_scales)
    weight = shift_weight(weight)
    got = lax.all_to_all(packed, GROUP, 0, 0, tiled=True)
    got, weight = lax.optimization_barrier((got, weight))
    other = swap(got[:, COUNT:])
    total, product, high = own_half(got, weight)
    share, back, high = other_half(got, other, weight, total, product, high)

    terms = lax.all_to_all(share, SPREAD, 0, 0, tiled=True)
    piece, peaks = reduce_terms(factor, terms, high)

    back, piece = lax.optimization_barrier((back, piece))
    back = lax.all_to_all(back, GROUP, 0, 0, tiled=True)
    peaks = over_shards(peaks)
    back, piece, peaks = lax.optimization_barrier((back, piece, peaks))
    input_grad = unpack(place, back)

    plane = lax.all_to_all(spread(piece, peaks), PLANE, 0, 0, tiled=True)
    weight_grad, peaks = merge(plane, swap(plane))
    return (input_grad, weight_grad, peaks)


def solution(mesh):
    fine = Mesh(mesh.devices.reshape(SIZES), AXES)
    return jax.shard_map(
        local,
        mesh=fine,
        in_specs=(P(AXES, None), P(AXES, None), P(("z", "xl"), None), P(("z", "xl"))),
        out_specs=(P(AXES, None), P(("z", "xl"), None), P()),
        check_vma=False,
    )
```

```python
import math

import jax
import jax.numpy as jnp
from jax import lax
from jax.experimental import pallas as pl
from jax.experimental.pallas import tpu as pltpu
from jax.sharding import Mesh
from jax.sharding import PartitionSpec as P

QBLOCK = 128
AXES = ("yh", "yl", "xh", "core", "z", "xl")
SIZES = (4, 2, 2, 2, 8, 2)
GROUP = ("yl", "xh", "core", "xl")
SPREAD = ("yh", "z")
PLANE = ("yh", "yl", "xh")
SHIFT = (0, 4, 1, 7, 2, 6, 3, 5)
BF16 = jnp.bfloat16
F32 = jnp.float32
COUNT = 128
HALF = COUNT // 2
KW = 512
PACK = COUNT + HALF
WIDE = KW + 128
PARAMS = pltpu.CompilerParams(vmem_limit_bytes=24 * 2**20)
VMEM = pl.BlockSpec(memory_space=pltpu.VMEM)
ANY = pl.BlockSpec(memory_space=pl.ANY)


def call(kernel, name, out_shape, in_specs, out_specs, flops, moved, **more):
    return pl.pallas_call(
        kernel,
        in_specs=in_specs,
        out_specs=out_specs,
        out_shape=out_shape,
        compiler_params=PARAMS,
        cost_estimate=pl.CostEstimate(flops=flops, bytes_accessed=moved, transcendentals=0),
        name=name,
        **more,
    )


def array(shape, dtype=BF16):
    return jax.ShapeDtypeStruct(shape, dtype)


def pack_kernel(tokens, keys, codes, scales, out, weight, columns, own, held, ready, scaled, factors, sems):
    loads = [
        pltpu.make_async_copy(tokens.at[:, pl.ds(z * 1024, 1024)], columns.at[z], sems.at[z]) for z in range(8)
    ]
    loads.append(pltpu.make_async_copy(keys, own, sems.at[8]))
    loads.append(pltpu.make_async_copy(codes, held, sems.at[9]))
    loads.append(pltpu.make_async_copy(scales, factors, sems.at[15]))
    for load in loads[8:] + loads[:8]:
        load.start()
    stores = []
    loads[9].wait()
    loads[10].wait()
    for block in range(4):
        rows = pl.ds(block * QBLOCK, QBLOCK)
        scaled[rows, :] = (held[rows, :].astype(F32) * factors[block]).astype(BF16)
    stores.append(pltpu.make_async_copy(scaled, weight, sems.at[10]))
    stores[-1].start()
    loads[8].wait()
    for part in range(16):
        core = part // 2 % 2
        ready[part, COUNT:PACK, :] = own[core * HALF : (core + 1) * HALF, :]
    low = lax.broadcasted_iota(jnp.int32, (HALF, 128), 1) < 64
    for m in range(4):
        loads[2 * m].wait()
        loads[2 * m + 1].wait()
        lanes = pl.ds(m * 128, 128)
        for t in range(4):
            for e in range(2):
                for half in range(2):
                    rows = pl.ds(half * HALF, HALF)
                    column = pl.ds(e * 512 + t * 128, 128)
                    even = columns[2 * m, rows, column]
                    odd = columns[2 * m + 1, rows, column]
                    for core in range(2):
                        first, second = (even, odd) if core == 0 else (odd, even)
                        at = HALF * (half ^ core)
                        ready[t * 4 + core * 2 + e, at : at + HALF, lanes] = jnp.where(low, first, second)
        stores.append(pltpu.make_async_copy(ready.at[:, :, lanes], out.at[:, :, lanes], sems.at[11 + m]))
        stores[-1].start()
    for store in stores:
        store.wait()


def hbm(x):
    return pltpu.with_memory_space_constraint(x, pltpu.HBM)


def pack(tokens, key_grad, codes, scales):
    return call(
        pack_kernel,
        "pack",
        [pltpu.HBM((16, PACK, KW), BF16), pltpu.HBM((512, KW), BF16)],
        [ANY] * 4,
        [ANY] * 2,
        0,
        9 * 2**20,
        scratch_shapes=[
            pltpu.VMEM((8, COUNT, 1024), BF16),
            pltpu.VMEM((COUNT, KW), BF16),
            pltpu.VMEM((512, KW), BF16),
            pltpu.VMEM((16, PACK, KW), BF16),
            pltpu.VMEM((512, KW), BF16),
            pltpu.SMEM((4,), F32),
            pltpu.SemaphoreType.DMA((16,)),
        ],
    )(hbm(tokens), hbm(key_grad), hbm(codes), hbm(scales))


def gradients(rows, keys):
    return lax.dot_general(
        rows.reshape(-1, KW), keys.reshape(-1, KW), (((0,), (0,)), ((), ())), preferred_element_type=F32
    )


def products(keys, weight):
    out = lax.dot_general(
        keys.reshape(-1, KW), weight, (((1,), (1,)), ((), ())), preferred_element_type=F32
    ).astype(BF16)
    return out, jnp.max(jnp.abs(out.astype(F32)).reshape(-1, 8, KW), axis=0)


def own_kernel(got, weight, total, product, high):
    total[...] = gradients(got[:, 0:HALF, :], got[:, COUNT:PACK, :])
    out, size = products(got[:, COUNT:PACK, :], weight[...])
    product[...] = out.reshape(16, HALF, KW)
    high[...] = size


def own_half(got, weight):
    return call(
        own_kernel,
        "own_half",
        [array((KW, KW), F32), array((16, HALF, KW)), array((8, KW), F32)],
        [VMEM] * 2,
        [VMEM] * 3,
        2**30,
        5 * 2**20,
    )(got, weight)


def other_kernel(got, other, weight, total, product, high_in, share, back, high, rest, sems):
    core = lax.axis_index("core")
    first = pltpu.make_async_copy(product, back.at[:, 0:HALF, :], sems.at[0])
    first.start()
    out, size = products(other[...], weight[...])
    rest[...] = out.reshape(16, HALF, KW)
    second = pltpu.make_async_copy(rest, back.at[:, HALF:COUNT, :], sems.at[1])
    second.start()
    high[...] = jnp.maximum(high_in[...], size)
    summed = (total[...] + gradients(got[:, HALF:COUNT, :], other[...])).astype(BF16)
    for m in range(4):
        for s in range(2):
            z = 2 * m + jnp.where(core == 0, s, 1 - s)
            for yh in range(4):
                row = m * 128 + s * 64 + yh * 16
                share[yh * 8 + z] = summed[row : row + 16, :]
    first.wait()
    second.wait()


def other_half(got, other, weight, total, product, high):
    return call(
        other_kernel,
        "other_half",
        [array((32, 16, KW)), pltpu.HBM((16, COUNT, KW), BF16), array((8, KW), F32)],
        [VMEM] * 6,
        [VMEM, ANY, VMEM],
        2**30,
        7 * 2**20,
        scratch_shapes=[pltpu.VMEM((16, HALF, KW), BF16), pltpu.SemaphoreType.DMA((2,))],
    )(got, other, weight, total, product, high)


def reduce_kernel(factor, terms, high, piece, peaks):
    total = terms[0].astype(F32)
    for k in range(1, 32):
        total += terms[k].astype(F32)
    rounded = (total * factor).astype(BF16)
    piece[...] = rounded
    first = jnp.max(high[...])
    second = jnp.max(jnp.abs(rounded.astype(F32)))
    lane = lax.broadcasted_iota(jnp.int32, (8, 128), 1)
    peaks[...] = jnp.where(lane < 64, first, second)


def reduce_terms(factor, terms, high):
    return call(
        lambda *refs: reduce_kernel(factor, *refs),
        "reduce_terms",
        [array((16, KW)), array((8, 128), F32)],
        [VMEM] * 2,
        [VMEM] * 2,
        2**18,
        2**20,
    )(terms, high)


def spread_kernel(piece, peaks, out):
    line = jnp.concatenate([peaks[...], peaks[...]], axis=0).astype(BF16)
    for k in range(16):
        out[k, :, 0:KW] = piece[...]
        out[k, :, KW:WIDE] = line


def spread(piece, peaks):
    return call(spread_kernel, "spread", array((16, 16, WIDE)), [VMEM] * 2, VMEM, 0, 2**19)(piece, peaks)


def unpack_kernel(back, out, sems):
    z = lax.axis_index("z")
    copies = []
    for q in range(8):
        place = lax.rem(z + SHIFT[q], 8) * 1024
        for e in range(2):
            lanes = pl.ds(pl.multiple_of(place + e * 512, 512), 512)
            for half in range(2):
                at = HALF * (half ^ (q % 2))
                copies.append(
                    pltpu.make_async_copy(
                        back.at[q * 2 + e, pl.ds(half * HALF, HALF), :],
                        out.at[pl.ds(at, HALF), lanes],
                        sems.at[len(copies)],
                    )
                )
                copies[-1].start()
    for copy in copies:
        copy.wait()


def unpack(back):
    return call(
        unpack_kernel,
        "unpack",
        pltpu.HBM((COUNT, 8192), BF16),
        [ANY],
        ANY,
        0,
        4 * 2**20,
        scratch_shapes=[pltpu.SemaphoreType.DMA((32,))],
    )(back)


def merge_kernel(mine, other, out, peaks):
    turn = lax.rem(lax.axis_index("core") + lax.axis_index("z"), 2)
    for source, s in ((mine, turn), (other, 1 - turn)):
        for yh in range(4):
            for t in range(4):
                row = pl.multiple_of(t * 128 + s * 64 + yh * 16, 16)
                out[pl.ds(row, 16), :] = source[yh * 4 + t, :, 0:KW].astype(F32)
    high = jnp.maximum(mine[:, :, KW:WIDE], other[:, :, KW:WIDE]).astype(F32)
    high = jnp.max(high, axis=0)
    low = lax.broadcasted_iota(jnp.int32, (16, 128), 1) < 64
    peaks[0] = jnp.max(jnp.where(low, high, 0.0))
    peaks[1] = jnp.max(jnp.where(low, 0.0, high))


def merge(mine, other):
    return call(
        merge_kernel,
        "merge",
        [array((512, KW), F32), array((2,), F32)],
        [VMEM] * 2,
        [VMEM, pl.BlockSpec(memory_space=pltpu.SMEM)],
        0,
        2 * 2**20,
    )(mine, other)


def from_ahead(x, axis, size, step):
    return lax.ppermute(x, axis, [((i + step) % size, i) for i in range(size)])


def over_shards(peaks):
    pairs = [(((z + 1) % 8) * 2 + 1 - xl, z * 2 + xl) for z in range(8) for xl in range(2)]
    near = [
        from_ahead(peaks, "z", 8, 1),
        from_ahead(peaks, "xl", 2, 1),
        lax.ppermute(peaks, ("z", "xl"), pairs),
    ]
    peaks = jnp.maximum(jnp.maximum(peaks, near[0]), jnp.maximum(near[1], near[2]))
    far = [from_ahead(peaks, "z", 8, step) for step in (2, 4, 6)]
    return jnp.maximum(jnp.maximum(peaks, far[0]), jnp.maximum(far[1], far[2]))


def swap(x):
    return from_ahead(x, "core", 2, 1)


def shift_weight(weight):
    pairs = [(q * 8 + (z + SHIFT[q]) % 8, q * 8 + z) for q in range(8) for z in range(8)]
    return lax.ppermute(weight, ("yl", "xh", "core", "z"), pairs)


def local(tokens, key_grad, weight_codes, block_scales):
    factor = 1.0 / math.sqrt(512 * COUNT)

    packed, weight = pack(tokens, key_grad, weight_codes, block_scales)
    weight = shift_weight(weight)
    got = lax.all_to_all(packed, GROUP, 0, 0, tiled=True)
    got, weight = lax.optimization_barrier((got, weight))
    other = swap(got[:, COUNT:])
    total, product, high = own_half(got, weight)
    share, back, high = other_half(got, other, weight, total, product, high)

    terms = lax.all_to_all(share, SPREAD, 0, 0, tiled=True)
    piece, peaks = reduce_terms(factor, terms, high)

    back, piece = lax.optimization_barrier((back, piece))
    back = lax.all_to_all(back, GROUP, 0, 0, tiled=True)
    peaks = over_shards(peaks)
    back, piece, peaks = lax.optimization_barrier((back, piece, peaks))
    input_grad = unpack(back)

    plane = lax.all_to_all(spread(piece, peaks), PLANE, 0, 0, tiled=True)
    weight_grad, peaks = merge(plane, swap(plane))
    return (input_grad, weight_grad, peaks)


def solution(mesh):
    fine = Mesh(mesh.devices.reshape(SIZES), AXES)
    return jax.shard_map(
        local,
        mesh=fine,
        in_specs=(P(AXES, None), P(AXES, None), P(("z", "xl"), None), P(("z", "xl"))),
        out_specs=(P(AXES, None), P(("z", "xl"), None), P()),
        check_vma=False,
    )
```

```python
import math

import jax
import jax.numpy as jnp
from jax import lax
from jax.experimental import pallas as pl
from jax.experimental.pallas import tpu as pltpu
from jax.sharding import Mesh
from jax.sharding import PartitionSpec as P

QBLOCK = 128
AXES = ("yh", "yl", "xh", "core", "z", "xl")
SIZES = (4, 2, 2, 2, 8, 2)
GROUP = ("yl", "xh", "core", "xl")
SPREAD = ("yh", "z")
PLANE = ("yh", "yl", "xh")
SHIFT = (0, 4, 1, 7, 2, 6, 3, 5)
BF16 = jnp.bfloat16
F32 = jnp.float32
COUNT = 128
HALF = COUNT // 2
KW = 512
PACK = COUNT + HALF
WIDE = KW + 128
PARAMS = pltpu.CompilerParams(vmem_limit_bytes=24 * 2**20)
VMEM = pl.BlockSpec(memory_space=pltpu.VMEM)
ANY = pl.BlockSpec(memory_space=pl.ANY)


def call(kernel, name, out_shape, in_specs, out_specs, flops, moved, **more):
    return pl.pallas_call(
        kernel,
        in_specs=in_specs,
        out_specs=out_specs,
        out_shape=out_shape,
        compiler_params=PARAMS,
        cost_estimate=pl.CostEstimate(flops=flops, bytes_accessed=moved, transcendentals=0),
        name=name,
        **more,
    )


def array(shape, dtype=BF16):
    return jax.ShapeDtypeStruct(shape, dtype)


def pack_kernel(tokens, keys, codes, scales, out, weight, columns, own, held, ready, scaled, factors, sems):
    loads = [
        pltpu.make_async_copy(tokens.at[:, pl.ds(z * 1024, 1024)], columns.at[z], sems.at[z]) for z in range(8)
    ]
    loads.append(pltpu.make_async_copy(keys, own, sems.at[8]))
    loads.append(pltpu.make_async_copy(codes, held, sems.at[9]))
    loads.append(pltpu.make_async_copy(scales, factors, sems.at[15]))
    for load in loads[8:] + loads[:8]:
        load.start()
    stores = []
    loads[9].wait()
    loads[10].wait()
    for block in range(4):
        rows = pl.ds(block * QBLOCK, QBLOCK)
        scaled[rows, :] = (held[rows, :].astype(F32) * factors[block]).astype(BF16)
    stores.append(pltpu.make_async_copy(scaled, weight, sems.at[10]))
    stores[-1].start()
    loads[8].wait()
    for part in range(16):
        core = part // 2 % 2
        ready[part, COUNT:PACK, :] = own[core * HALF : (core + 1) * HALF, :]
    low = lax.broadcasted_iota(jnp.int32, (HALF, 128), 1) < 64
    for m in range(4):
        loads[2 * m].wait()
        loads[2 * m + 1].wait()
        lanes = pl.ds(m * 128, 128)
        for t in range(4):
            for e in range(2):
                for half in range(2):
                    rows = pl.ds(half * HALF, HALF)
                    column = pl.ds(e * 512 + t * 128, 128)
                    even = columns[2 * m, rows, column]
                    odd = columns[2 * m + 1, rows, column]
                    for core in range(2):
                        first, second = (even, odd) if core == 0 else (odd, even)
                        at = HALF * (half ^ core)
                        ready[t * 4 + core * 2 + e, at : at + HALF, lanes] = jnp.where(low, first, second)
        stores.append(pltpu.make_async_copy(ready.at[:, :, lanes], out.at[:, :, lanes], sems.at[11 + m]))
        stores[-1].start()
    for store in stores:
        store.wait()


def hbm(x):
    return pltpu.with_memory_space_constraint(x, pltpu.HBM)


def pack(tokens, key_grad, codes, scales):
    return call(
        pack_kernel,
        "pack",
        [pltpu.HBM((16, PACK, KW), BF16), pltpu.HBM((512, KW), BF16)],
        [ANY] * 4,
        [ANY] * 2,
        0,
        9 * 2**20,
        scratch_shapes=[
            pltpu.VMEM((8, COUNT, 1024), BF16),
            pltpu.VMEM((COUNT, KW), BF16),
            pltpu.VMEM((512, KW), BF16),
            pltpu.VMEM((16, PACK, KW), BF16),
            pltpu.VMEM((512, KW), BF16),
            pltpu.SMEM((4,), F32),
            pltpu.SemaphoreType.DMA((16,)),
        ],
    )(hbm(tokens), hbm(key_grad), hbm(codes), hbm(scales))


def gradients(rows, keys):
    return lax.dot_general(
        rows.reshape(-1, KW), keys.reshape(-1, KW), (((0,), (0,)), ((), ())), preferred_element_type=F32
    )


def products(keys, weight):
    out = lax.dot_general(
        keys.reshape(-1, KW), weight, (((1,), (1,)), ((), ())), preferred_element_type=F32
    ).astype(BF16)
    return out, jnp.max(jnp.abs(out.astype(F32)).reshape(-1, 8, KW), axis=0)


def own_kernel(got, total, mine, sem):
    copy = pltpu.make_async_copy(got.at[:, pl.ds(COUNT, HALF), :], mine, sem)
    copy.start()
    total[...] = gradients(got[:, 0:HALF, :], got[:, COUNT:PACK, :])
    copy.wait()


def own_half(got):
    return call(
        own_kernel,
        "own_half",
        [array((KW, KW), F32), pltpu.HBM((16, HALF, KW), BF16)],
        [VMEM],
        [VMEM, ANY],
        2**29,
        4 * 2**20,
        scratch_shapes=[pltpu.SemaphoreType.DMA],
    )(got)


def other_kernel(got, other, total, share, kept, chunks, sems):
    core = lax.axis_index("core")
    keep = pltpu.make_async_copy(other, kept, sems.at[0])
    keep.start()
    summed = (total[...] + gradients(got[:, HALF:COUNT, :], other[...])).astype(BF16)
    for m in range(4):
        for s in range(2):
            z = 2 * m + jnp.where(core == 0, s, 1 - s)
            for yh in range(4):
                row = m * 128 + s * 64 + yh * 16
                chunks[yh * 8 + z] = summed[row : row + 16, :]
    store = pltpu.make_async_copy(chunks, share, sems.at[1])
    store.start()
    keep.wait()
    store.wait()


def other_half(got, other, total):
    return call(
        other_kernel,
        "other_half",
        [pltpu.HBM((32, 16, KW), BF16), pltpu.HBM((16, HALF, KW), BF16)],
        [VMEM] * 3,
        [ANY] * 2,
        2**29,
        4 * 2**20,
        scratch_shapes=[pltpu.VMEM((32, 16, KW), BF16), pltpu.SemaphoreType.DMA((2,))],
    )(got, other, total)


def product_kernel(mine, other, weight, back, high, keys, scaled, rest, sems):
    loads = [
        pltpu.make_async_copy(weight, scaled, sems.at[0]),
        pltpu.make_async_copy(mine, keys.at[0], sems.at[1]),
        pltpu.make_async_copy(other, keys.at[1], sems.at[2]),
    ]
    for load in loads:
        load.start()
    loads[0].wait()
    stores = []
    sizes = []
    for half in range(2):
        loads[1 + half].wait()
        out, size = products(keys[half], scaled[...])
        sizes.append(size)
        rest[half] = out.reshape(16, HALF, KW)
        rows = pl.ds(half * HALF, HALF)
        stores.append(pltpu.make_async_copy(rest.at[half], back.at[:, rows, :], sems.at[3 + half]))
        stores[-1].start()
    high[...] = jnp.maximum(sizes[0], sizes[1])
    for store in stores:
        store.wait()


def product(mine, other, weight):
    return call(
        product_kernel,
        "product",
        [pltpu.HBM((16, COUNT, KW), BF16), array((8, KW), F32)],
        [ANY] * 3,
        [ANY, VMEM],
        2**30,
        5 * 2**20,
        scratch_shapes=[
            pltpu.VMEM((2, 16, HALF, KW), BF16),
            pltpu.VMEM((KW, KW), BF16),
            pltpu.VMEM((2, 16, HALF, KW), BF16),
            pltpu.SemaphoreType.DMA((5,)),
        ],
    )(hbm(mine), hbm(other), hbm(weight))


def reduce_kernel(factor, terms, high, piece, peaks):
    total = terms[0].astype(F32)
    for k in range(1, 32):
        total += terms[k].astype(F32)
    rounded = (total * factor).astype(BF16)
    piece[...] = rounded
    first = jnp.max(high[...])
    second = jnp.max(jnp.abs(rounded.astype(F32)))
    lane = lax.broadcasted_iota(jnp.int32, (8, 128), 1)
    peaks[...] = jnp.where(lane < 64, first, second)


def reduce_terms(factor, terms, high):
    return call(
        lambda *refs: reduce_kernel(factor, *refs),
        "reduce_terms",
        [array((16, KW)), array((8, 128), F32)],
        [VMEM] * 2,
        [VMEM] * 2,
        2**18,
        2**20,
    )(terms, high)


def spread_kernel(piece, peaks, out):
    line = jnp.concatenate([peaks[...], peaks[...]], axis=0).astype(BF16)
    for k in range(16):
        out[k, :, 0:KW] = piece[...]
        out[k, :, KW:WIDE] = line


def spread(piece, peaks):
    return call(spread_kernel, "spread", array((16, 16, WIDE)), [VMEM] * 2, VMEM, 0, 2**19)(piece, peaks)


def unpack_kernel(back, out, sems):
    z = lax.axis_index("z")
    copies = []
    for q in range(8):
        place = lax.rem(z + SHIFT[q], 8) * 1024
        for e in range(2):
            lanes = pl.ds(pl.multiple_of(place + e * 512, 512), 512)
            for half in range(2):
                at = HALF * (half ^ (q % 2))
                copies.append(
                    pltpu.make_async_copy(
                        back.at[q * 2 + e, pl.ds(half * HALF, HALF), :],
                        out.at[pl.ds(at, HALF), lanes],
                        sems.at[len(copies)],
                    )
                )
                copies[-1].start()
    for copy in copies:
        copy.wait()


def unpack(back):
    return call(
        unpack_kernel,
        "unpack",
        pltpu.HBM((COUNT, 8192), BF16),
        [ANY],
        ANY,
        0,
        4 * 2**20,
        scratch_shapes=[pltpu.SemaphoreType.DMA((32,))],
    )(back)


def peaks_kernel(mine, other, out):
    high = jnp.maximum(mine[:, :, KW:WIDE], other[:, :, KW:WIDE]).astype(F32)
    high = jnp.max(high, axis=0)
    out[...] = jnp.maximum(high[0:8], high[8:16])


def peaks_of(mine, other):
    return call(peaks_kernel, "peaks_of", array((8, 128), F32), [VMEM] * 2, VMEM, 2**15, 2**17)(mine, other)


def last_kernel(a, b, out):
    high = jnp.maximum(a[...], b[...])
    low = lax.broadcasted_iota(jnp.int32, (8, 128), 1) < 64
    out[0] = jnp.max(jnp.where(low, high, 0.0))
    out[1] = jnp.max(jnp.where(low, 0.0, high))


def last(a, b):
    smem = pl.BlockSpec(memory_space=pltpu.SMEM)
    return call(last_kernel, "last", array((2,), F32), [VMEM] * 2, smem, 2**12, 2**13)(a, b)


def merge_kernel(mine, other, out):
    turn = lax.rem(lax.axis_index("core") + lax.axis_index("z"), 2)
    for source, s in ((mine, turn), (other, 1 - turn)):
        for yh in range(4):
            for t in range(4):
                row = pl.multiple_of(t * 128 + s * 64 + yh * 16, 16)
                out[pl.ds(row, 16), :] = source[yh * 4 + t, :, 0:KW].astype(F32)


def merge(mine, other):
    return call(merge_kernel, "merge", array((512, KW), F32), [VMEM] * 2, VMEM, 0, 2 * 2**20)(mine, other)


def from_ahead(x, axis, size, step):
    return lax.ppermute(x, axis, [((i + step) % size, i) for i in range(size)])


def with_neighbours(peaks, step):
    ahead = from_ahead(peaks, "z", 8, step)
    behind = from_ahead(peaks, "z", 8, 8 - step)
    return jnp.maximum(peaks, jnp.maximum(ahead, behind))


def swap(x):
    return from_ahead(x, "core", 2, 1)


def shift_weight(weight):
    pairs = [(q * 8 + (z + SHIFT[q]) % 8, q * 8 + z) for q in range(8) for z in range(8)]
    return lax.ppermute(weight, ("yl", "xh", "core", "z"), pairs)


def local(tokens, key_grad, weight_codes, block_scales):
    factor = 1.0 / math.sqrt(512 * COUNT)

    packed, weight = pack(tokens, key_grad, weight_codes, block_scales)
    weight = shift_weight(weight)
    got = lax.all_to_all(packed, GROUP, 0, 0, tiled=True)
    got, weight = lax.optimization_barrier((got, weight))
    total, mine = own_half(got)
    share, other = other_half(got, swap(got[:, COUNT:]), total)
    back, high = product(mine, other, weight)

    terms = lax.all_to_all(share, SPREAD, 0, 0, tiled=True)
    piece, peaks = reduce_terms(factor, terms, high)

    plane = lax.all_to_all(spread(piece, peaks), PLANE, 0, 0, tiled=True)

    back, plane = lax.optimization_barrier((back, plane))
    back = lax.all_to_all(back, GROUP, 0, 0, tiled=True)
    other = swap(plane)
    peaks = with_neighbours(peaks_of(plane, other), 1)
    weight_grad = merge(plane, other)
    weight_grad, peaks = lax.optimization_barrier((weight_grad, peaks))
    peaks = with_neighbours(peaks, 3)
    input_grad = unpack(back)
    input_grad, across = lax.optimization_barrier((input_grad, from_ahead(peaks, "xl", 2, 1)))
    return (input_grad, weight_grad, last(peaks, across))


def solution(mesh):
    fine = Mesh(mesh.devices.reshape(SIZES), AXES)
    return jax.shard_map(
        local,
        mesh=fine,
        in_specs=(P(AXES, None), P(AXES, None), P(("z", "xl"), None), P(("z", "xl"))),
        out_specs=(P(AXES, None), P(("z", "xl"), None), P()),
        check_vma=False,
    )
```

```python
import math

import jax
import jax.numpy as jnp
from jax import lax
from jax.experimental import pallas as pl
from jax.experimental.pallas import tpu as pltpu
from jax.sharding import Mesh
from jax.sharding import PartitionSpec as P

QBLOCK = 128
AXES = ("yh", "yl", "xh", "core", "z", "xl")
SIZES = (4, 2, 2, 2, 8, 2)
GROUP = ("yl", "xh", "core", "xl")
SPREAD = ("yh", "z")
PLANE = ("xh", "yh", "yl")
SHIFT = (0, 4, 1, 7, 2, 6, 3, 5)
BF16 = jnp.bfloat16
F32 = jnp.float32
COUNT = 128
HALF = COUNT // 2
KW = 512
PACK = COUNT + HALF
WIDE = KW + 128
PARAMS = pltpu.CompilerParams(vmem_limit_bytes=24 * 2**20)
VMEM = pl.BlockSpec(memory_space=pltpu.VMEM)
ANY = pl.BlockSpec(memory_space=pl.ANY)


def call(kernel, name, out_shape, in_specs, out_specs, flops, moved, **more):
    return pl.pallas_call(
        kernel,
        in_specs=in_specs,
        out_specs=out_specs,
        out_shape=out_shape,
        compiler_params=PARAMS,
        cost_estimate=pl.CostEstimate(flops=flops, bytes_accessed=moved, transcendentals=0),
        name=name,
        **more,
    )


def array(shape, dtype=BF16):
    return jax.ShapeDtypeStruct(shape, dtype)


def pack_kernel(tokens, keys, codes, scales, out, weight, columns, own, held, ready, scaled, factors, sems):
    loads = [
        pltpu.make_async_copy(tokens.at[:, pl.ds(z * 1024, 1024)], columns.at[z], sems.at[z]) for z in range(8)
    ]
    loads.append(pltpu.make_async_copy(keys, own, sems.at[8]))
    loads.append(pltpu.make_async_copy(codes, held, sems.at[9]))
    loads.append(pltpu.make_async_copy(scales, factors, sems.at[15]))
    for load in loads[8:] + loads[:8]:
        load.start()
    stores = []
    loads[9].wait()
    loads[10].wait()
    for block in range(4):
        rows = pl.ds(block * QBLOCK, QBLOCK)
        scaled[rows, :] = (held[rows, :].astype(F32) * factors[block]).astype(BF16)
    stores.append(pltpu.make_async_copy(scaled, weight, sems.at[10]))
    stores[-1].start()
    loads[8].wait()
    for part in range(16):
        core = part // 2 % 2
        ready[part, COUNT:PACK, :] = own[core * HALF : (core + 1) * HALF, :]
    low = lax.broadcasted_iota(jnp.int32, (HALF, 128), 1) < 64
    for m in range(4):
        loads[2 * m].wait()
        loads[2 * m + 1].wait()
        lanes = pl.ds(m * 128, 128)
        for t in range(4):
            for e in range(2):
                for half in range(2):
                    rows = pl.ds(half * HALF, HALF)
                    column = pl.ds(e * 512 + t * 128, 128)
                    even = columns[2 * m, rows, column]
                    odd = columns[2 * m + 1, rows, column]
                    for core in range(2):
                        first, second = (even, odd) if core == 0 else (odd, even)
                        at = HALF * (half ^ core)
                        ready[t * 4 + core * 2 + e, at : at + HALF, lanes] = jnp.where(low, first, second)
        stores.append(pltpu.make_async_copy(ready.at[:, :, lanes], out.at[:, :, lanes], sems.at[11 + m]))
        stores[-1].start()
    for store in stores:
        store.wait()


def hbm(x):
    return pltpu.with_memory_space_constraint(x, pltpu.HBM)


def pack(tokens, key_grad, codes, scales):
    return call(
        pack_kernel,
        "pack",
        [pltpu.HBM((16, PACK, KW), BF16), pltpu.HBM((512, KW), BF16)],
        [ANY] * 4,
        [ANY] * 2,
        0,
        9 * 2**20,
        scratch_shapes=[
            pltpu.VMEM((8, COUNT, 1024), BF16),
            pltpu.VMEM((COUNT, KW), BF16),
            pltpu.VMEM((512, KW), BF16),
            pltpu.VMEM((16, PACK, KW), BF16),
            pltpu.VMEM((512, KW), BF16),
            pltpu.SMEM((4,), F32),
            pltpu.SemaphoreType.DMA((16,)),
        ],
    )(hbm(tokens), hbm(key_grad), hbm(codes), hbm(scales))


def gradients(rows, keys):
    return lax.dot_general(
        rows.reshape(-1, KW), keys.reshape(-1, KW), (((0,), (0,)), ((), ())), preferred_element_type=F32
    )


def products(keys, weight):
    out = lax.dot_general(
        keys.reshape(-1, KW), weight, (((1,), (1,)), ((), ())), preferred_element_type=F32
    ).astype(BF16)
    return out, jnp.max(jnp.abs(out.astype(F32)).reshape(-1, 8, KW), axis=0)


def own_kernel(got, total, mine, sem):
    copy = pltpu.make_async_copy(got.at[:, pl.ds(COUNT, HALF), :], mine, sem)
    copy.start()
    total[...] = gradients(got[:, 0:HALF, :], got[:, COUNT:PACK, :])
    copy.wait()


def own_half(got):
    return call(
        own_kernel,
        "own_half",
        [array((KW, KW), F32), pltpu.HBM((16, HALF, KW), BF16)],
        [VMEM],
        [VMEM, ANY],
        2**29,
        4 * 2**20,
        scratch_shapes=[pltpu.SemaphoreType.DMA],
    )(got)


def other_kernel(got, other, total, share, kept, chunks, sems):
    core = lax.axis_index("core")
    keep = pltpu.make_async_copy(other, kept, sems.at[0])
    keep.start()
    summed = (total[...] + gradients(got[:, HALF:COUNT, :], other[...])).astype(BF16)
    for m in range(4):
        for s in range(2):
            z = 2 * m + jnp.where(core == 0, s, 1 - s)
            for yh in range(4):
                row = m * 128 + s * 64 + yh * 16
                chunks[yh * 8 + z] = summed[row : row + 16, :]
    store = pltpu.make_async_copy(chunks, share, sems.at[1])
    store.start()
    keep.wait()
    store.wait()


def other_half(got, other, total):
    return call(
        other_kernel,
        "other_half",
        [pltpu.HBM((32, 16, KW), BF16), pltpu.HBM((16, HALF, KW), BF16)],
        [VMEM] * 3,
        [ANY] * 2,
        2**29,
        4 * 2**20,
        scratch_shapes=[pltpu.VMEM((32, 16, KW), BF16), pltpu.SemaphoreType.DMA((2,))],
    )(got, other, total)


def product_kernel(mine, other, weight, back, high, keys, scaled, rest, sems):
    loads = [
        pltpu.make_async_copy(weight, scaled, sems.at[0]),
        pltpu.make_async_copy(mine, keys.at[0], sems.at[1]),
        pltpu.make_async_copy(other, keys.at[1], sems.at[2]),
    ]
    for load in loads:
        load.start()
    loads[0].wait()
    stores = []
    sizes = []
    for half in range(2):
        loads[1 + half].wait()
        out, size = products(keys[half], scaled[...])
        sizes.append(size)
        rest[half] = out.reshape(16, HALF, KW)
        rows = pl.ds(half * HALF, HALF)
        stores.append(pltpu.make_async_copy(rest.at[half], back.at[:, rows, :], sems.at[3 + half]))
        stores[-1].start()
    high[...] = jnp.maximum(sizes[0], sizes[1])
    for store in stores:
        store.wait()


def product(mine, other, weight):
    return call(
        product_kernel,
        "product",
        [pltpu.HBM((16, COUNT, KW), BF16), array((8, KW), F32)],
        [ANY] * 3,
        [ANY, VMEM],
        2**30,
        5 * 2**20,
        scratch_shapes=[
            pltpu.VMEM((2, 16, HALF, KW), BF16),
            pltpu.VMEM((KW, KW), BF16),
            pltpu.VMEM((2, 16, HALF, KW), BF16),
            pltpu.SemaphoreType.DMA((5,)),
        ],
    )(hbm(mine), hbm(other), hbm(weight))


def reduce_kernel(factor, terms, high, piece, peaks):
    total = terms[0].astype(F32)
    for k in range(1, 32):
        total += terms[k].astype(F32)
    rounded = (total * factor).astype(BF16)
    piece[...] = rounded
    first = jnp.max(high[...])
    second = jnp.max(jnp.abs(rounded.astype(F32)))
    lane = lax.broadcasted_iota(jnp.int32, (8, 128), 1)
    peaks[...] = jnp.where(lane < 64, first, second)


def reduce_terms(factor, terms, high):
    return call(
        lambda *refs: reduce_kernel(factor, *refs),
        "reduce_terms",
        [array((16, KW)), array((8, 128), F32)],
        [VMEM] * 2,
        [VMEM] * 2,
        2**18,
        2**20,
    )(terms, high)


def spread_kernel(piece, peaks, out):
    line = jnp.concatenate([peaks[...], peaks[...]], axis=0).astype(BF16)
    for k in range(16):
        out[k, :, 0:KW] = piece[...]
        out[k, :, KW:WIDE] = line


def spread(piece, peaks):
    return call(spread_kernel, "spread", array((16, 16, WIDE)), [VMEM] * 2, VMEM, 0, 2**19)(piece, peaks)


def unpack_kernel(back, out, sems):
    z = lax.axis_index("z")
    copies = []
    for q in range(8):
        place = lax.rem(z + SHIFT[q], 8) * 1024
        for e in range(2):
            lanes = pl.ds(pl.multiple_of(place + e * 512, 512), 512)
            for half in range(2):
                at = HALF * (half ^ (q % 2))
                copies.append(
                    pltpu.make_async_copy(
                        back.at[q * 2 + e, pl.ds(half * HALF, HALF), :],
                        out.at[pl.ds(at, HALF), lanes],
                        sems.at[len(copies)],
                    )
                )
                copies[-1].start()
    for copy in copies:
        copy.wait()


def unpack(back):
    return call(
        unpack_kernel,
        "unpack",
        pltpu.HBM((COUNT, 8192), BF16),
        [ANY],
        ANY,
        0,
        4 * 2**20,
        scratch_shapes=[pltpu.SemaphoreType.DMA((32,))],
    )(back)


def peaks_kernel(mine, other, out):
    high = jnp.maximum(mine[:, :, KW:WIDE], other[:, :, KW:WIDE]).astype(F32)
    high = jnp.max(high, axis=0)
    out[...] = jnp.maximum(high[0:8], high[8:16])


def peaks_of(mine, other):
    return call(peaks_kernel, "peaks_of", array((8, 128), F32), [VMEM] * 2, VMEM, 2**15, 2**17)(mine, other)


def last_kernel(a, b, out):
    high = jnp.maximum(a[...], b[...])
    low = lax.broadcasted_iota(jnp.int32, (8, 128), 1) < 64
    out[0] = jnp.max(jnp.where(low, high, 0.0))
    out[1] = jnp.max(jnp.where(low, 0.0, high))


def last(a, b):
    smem = pl.BlockSpec(memory_space=pltpu.SMEM)
    return call(last_kernel, "last", array((2,), F32), [VMEM] * 2, smem, 2**12, 2**13)(a, b)


def merge_kernel(mine, other, out):
    turn = lax.rem(lax.axis_index("core") + lax.axis_index("z"), 2)
    for source, s in ((mine, turn), (other, 1 - turn)):
        for yh in range(4):
            for t in range(4):
                row = pl.multiple_of(t * 128 + s * 64 + yh * 16, 16)
                out[pl.ds(row, 16), :] = source[t % 2 * 8 + yh * 2 + t // 2, :, 0:KW].astype(F32)


def merge(mine, other):
    return call(merge_kernel, "merge", array((512, KW), F32), [VMEM] * 2, VMEM, 0, 2 * 2**20)(mine, other)


def from_ahead(x, axis, size, step):
    return lax.ppermute(x, axis, [((i + step) % size, i) for i in range(size)])


def with_neighbours(peaks, step):
    ahead = from_ahead(peaks, "z", 8, step)
    behind = from_ahead(peaks, "z", 8, 8 - step)
    return jnp.maximum(peaks, jnp.maximum(ahead, behind))


def swap(x):
    return from_ahead(x, "core", 2, 1)


def shift_weight(weight):
    pairs = [(q * 8 + (z + SHIFT[q]) % 8, q * 8 + z) for q in range(8) for z in range(8)]
    return lax.ppermute(weight, ("yl", "xh", "core", "z"), pairs)


def local(tokens, key_grad, weight_codes, block_scales):
    factor = 1.0 / math.sqrt(512 * COUNT)

    packed, weight = pack(tokens, key_grad, weight_codes, block_scales)
    weight = shift_weight(weight)
    got = lax.all_to_all(packed, GROUP, 0, 0, tiled=True)
    got, weight = lax.optimization_barrier((got, weight))
    total, mine = own_half(got)
    share, other = other_half(got, swap(got[:, COUNT:]), total)
    back, high = product(mine, other, weight)

    terms = lax.all_to_all(share, SPREAD, 0, 0, tiled=True)
    piece, peaks = reduce_terms(factor, terms, high)

    plane = lax.all_to_all(spread(piece, peaks), PLANE, 0, 0, tiled=True)

    back, plane = lax.optimization_barrier((back, plane))
    back = lax.all_to_all(back, GROUP, 0, 0, tiled=True)
    other = swap(plane)
    peaks = with_neighbours(peaks_of(plane, other), 1)
    weight_grad = merge(plane, other)
    weight_grad, peaks = lax.optimization_barrier((weight_grad, peaks))
    peaks = with_neighbours(peaks, 3)
    input_grad = unpack(back)
    input_grad, across = lax.optimization_barrier((input_grad, from_ahead(peaks, "xl", 2, 1)))
    return (input_grad, weight_grad, last(peaks, across))


def solution(mesh):
    fine = Mesh(mesh.devices.reshape(SIZES), AXES)
    return jax.shard_map(
        local,
        mesh=fine,
        in_specs=(P(AXES, None), P(AXES, None), P(("z", "xl"), None), P(("z", "xl"))),
        out_specs=(P(AXES, None), P(("z", "xl"), None), P()),
        check_vma=False,
    )
```

```python
import math

import jax
import jax.numpy as jnp
from jax import lax
from jax.experimental import pallas as pl
from jax.experimental.pallas import tpu as pltpu
from jax.sharding import Mesh
from jax.sharding import PartitionSpec as P

QBLOCK = 128
AXES = ("yh", "yl", "xh", "core", "z", "xl")
SIZES = (4, 2, 2, 2, 8, 2)
GROUP = ("yl", "xh", "core", "xl")
SPREAD = ("yh", "z")
PLANE = ("xh", "yh", "yl")
SHIFT = (0, 4, 1, 7, 2, 6, 3, 5)
BF16 = jnp.bfloat16
F32 = jnp.float32
COUNT = 128
HALF = COUNT // 2
KW = 512
PACK = COUNT + HALF
WIDE = KW + 128
PARAMS = pltpu.CompilerParams(vmem_limit_bytes=24 * 2**20)
VMEM = pl.BlockSpec(memory_space=pltpu.VMEM)
ANY = pl.BlockSpec(memory_space=pl.ANY)


def call(kernel, name, out_shape, in_specs, out_specs, flops, moved, **more):
    return pl.pallas_call(
        kernel,
        in_specs=in_specs,
        out_specs=out_specs,
        out_shape=out_shape,
        compiler_params=PARAMS,
        cost_estimate=pl.CostEstimate(flops=flops, bytes_accessed=moved, transcendentals=0),
        name=name,
        **more,
    )


def array(shape, dtype=BF16):
    return jax.ShapeDtypeStruct(shape, dtype)


def pack_kernel(tokens, keys, codes, scales, out, weight, columns, own, held, ready, scaled, factors, sems):
    loads = [
        pltpu.make_async_copy(tokens.at[:, pl.ds(z * 1024, 1024)], columns.at[z], sems.at[z]) for z in range(8)
    ]
    loads.append(pltpu.make_async_copy(keys, own, sems.at[8]))
    loads.append(pltpu.make_async_copy(codes, held, sems.at[9]))
    loads.append(pltpu.make_async_copy(scales, factors, sems.at[15]))
    for load in loads[8:] + loads[:8]:
        load.start()
    stores = []
    loads[9].wait()
    loads[10].wait()
    for block in range(4):
        rows = pl.ds(block * QBLOCK, QBLOCK)
        scaled[rows, :] = (held[rows, :].astype(F32) * factors[block]).astype(BF16)
    stores.append(pltpu.make_async_copy(scaled, weight, sems.at[10]))
    stores[-1].start()
    loads[8].wait()
    for part in range(16):
        core = part // 2 % 2
        ready[part, COUNT:PACK, :] = own[core * HALF : (core + 1) * HALF, :]
    low = lax.broadcasted_iota(jnp.int32, (HALF, 128), 1) < 64
    for m in range(4):
        loads[2 * m].wait()
        loads[2 * m + 1].wait()
        lanes = pl.ds(m * 128, 128)
        for t in range(4):
            for e in range(2):
                for half in range(2):
                    rows = pl.ds(half * HALF, HALF)
                    column = pl.ds(e * 512 + t * 128, 128)
                    even = columns[2 * m, rows, column]
                    odd = columns[2 * m + 1, rows, column]
                    for core in range(2):
                        first, second = (even, odd) if core == 0 else (odd, even)
                        at = HALF * (half ^ core)
                        ready[t * 4 + half * 2 + e, at : at + HALF, lanes] = jnp.where(low, first, second)
        stores.append(pltpu.make_async_copy(ready.at[:, :, lanes], out.at[:, :, lanes], sems.at[11 + m]))
        stores[-1].start()
    for store in stores:
        store.wait()


def hbm(x):
    return pltpu.with_memory_space_constraint(x, pltpu.HBM)


def pack(tokens, key_grad, codes, scales):
    return call(
        pack_kernel,
        "pack",
        [pltpu.HBM((16, PACK, KW), BF16), pltpu.HBM((512, KW), BF16)],
        [ANY] * 4,
        [ANY] * 2,
        0,
        9 * 2**20,
        scratch_shapes=[
            pltpu.VMEM((8, COUNT, 1024), BF16),
            pltpu.VMEM((COUNT, KW), BF16),
            pltpu.VMEM((512, KW), BF16),
            pltpu.VMEM((16, PACK, KW), BF16),
            pltpu.VMEM((512, KW), BF16),
            pltpu.SMEM((4,), F32),
            pltpu.SemaphoreType.DMA((16,)),
        ],
    )(hbm(tokens), hbm(key_grad), hbm(codes), hbm(scales))


def gradients(rows, keys):
    return lax.dot_general(
        rows.reshape(-1, KW), keys.reshape(-1, KW), (((0,), (0,)), ((), ())), preferred_element_type=F32
    )


def products(keys, weight):
    out = lax.dot_general(
        keys.reshape(-1, KW), weight, (((1,), (1,)), ((), ())), preferred_element_type=F32
    ).astype(BF16)
    return out, jnp.max(jnp.abs(out.astype(F32)).reshape(-1, 8, KW), axis=0)


def away_kernel(got, out):
    out[...] = gradients(got[:, HALF:COUNT, :], got[:, COUNT:PACK, :]).astype(BF16)


def away(got):
    return call(away_kernel, "away", array((KW, KW)), [VMEM], VMEM, 2**29, 3 * 2**20)(got)


def home_kernel(got, total, mine, sem):
    copy = pltpu.make_async_copy(got.at[:, pl.ds(COUNT, HALF), :], mine, sem)
    copy.start()
    total[...] = gradients(got[:, 0:HALF, :], got[:, COUNT:PACK, :])
    copy.wait()


def home(got):
    return call(
        home_kernel,
        "home",
        [array((KW, KW), F32), pltpu.HBM((16, HALF, KW), BF16)],
        [VMEM],
        [VMEM, ANY],
        2**29,
        4 * 2**20,
        scratch_shapes=[pltpu.SemaphoreType.DMA],
    )(got)


def join_kernel(total, other, share, chunks, sem):
    core = lax.axis_index("core")
    summed = (total[...] + other[...].astype(F32)).astype(BF16)
    for m in range(4):
        for s in range(2):
            z = 2 * m + jnp.where(core == 0, s, 1 - s)
            for yh in range(4):
                row = m * 128 + s * 64 + yh * 16
                chunks[yh * 8 + z] = summed[row : row + 16, :]
    store = pltpu.make_async_copy(chunks, share, sem)
    store.start()
    store.wait()


def join(total, other):
    return call(
        join_kernel,
        "join",
        pltpu.HBM((32, 16, KW), BF16),
        [VMEM] * 2,
        ANY,
        2**18,
        2**21,
        scratch_shapes=[pltpu.VMEM((32, 16, KW), BF16), pltpu.SemaphoreType.DMA],
    )(total, other)


def product_kernel(mine, weight, across, back, high, keys, scaled, rest, sems):
    loads = [
        pltpu.make_async_copy(mine, keys, sems.at[0]),
        pltpu.make_async_copy(weight, scaled.at[0], sems.at[1]),
        pltpu.make_async_copy(across, scaled.at[1], sems.at[2]),
    ]
    for load in loads:
        load.start()
    loads[0].wait()
    stores = []
    sizes = []
    for which in range(2):
        loads[1 + which].wait()
        out, size = products(keys[...], scaled[which])
        sizes.append(size)
        rest[which] = out.reshape(16, HALF, KW)
        rows = pl.ds(which * HALF, HALF)
        stores.append(pltpu.make_async_copy(rest.at[which], back.at[:, rows, :], sems.at[3 + which]))
        stores[-1].start()
    high[...] = jnp.maximum(sizes[0], sizes[1])
    for store in stores:
        store.wait()


def product(mine, weight, across):
    return call(
        product_kernel,
        "product",
        [pltpu.HBM((16, COUNT, KW), BF16), array((8, KW), F32)],
        [ANY] * 3,
        [ANY, VMEM],
        2**30,
        5 * 2**20,
        scratch_shapes=[
            pltpu.VMEM((16, HALF, KW), BF16),
            pltpu.VMEM((2, KW, KW), BF16),
            pltpu.VMEM((2, 16, HALF, KW), BF16),
            pltpu.SemaphoreType.DMA((5,)),
        ],
    )(hbm(mine), hbm(weight), hbm(across))


def reduce_kernel(factor, terms, high, piece, peaks):
    total = terms[0].astype(F32)
    for k in range(1, 32):
        total += terms[k].astype(F32)
    rounded = (total * factor).astype(BF16)
    piece[...] = rounded
    first = jnp.max(high[...])
    second = jnp.max(jnp.abs(rounded.astype(F32)))
    lane = lax.broadcasted_iota(jnp.int32, (8, 128), 1)
    peaks[...] = jnp.where(lane < 64, first, second)


def reduce_terms(factor, terms, high):
    return call(
        lambda *refs: reduce_kernel(factor, *refs),
        "reduce_terms",
        [array((16, KW)), array((8, 128), F32)],
        [VMEM] * 2,
        [VMEM] * 2,
        2**18,
        2**20,
    )(terms, high)


def spread_kernel(piece, peaks, out):
    line = jnp.concatenate([peaks[...], peaks[...]], axis=0).astype(BF16)
    for k in range(16):
        out[k, :, 0:KW] = piece[...]
        out[k, :, KW:WIDE] = line


def spread(piece, peaks):
    return call(spread_kernel, "spread", array((16, 16, WIDE)), [VMEM] * 2, VMEM, 0, 2**19)(piece, peaks)


def unpack_kernel(back, out, sems):
    z = lax.axis_index("z")
    copies = []
    for q in range(8):
        core = q % 2
        for which in range(2):
            place = lax.rem(z + SHIFT[q ^ which], 8) * 1024
            for e in range(2):
                lanes = pl.ds(pl.multiple_of(place + e * 512, 512), 512)
                copies.append(
                    pltpu.make_async_copy(
                        back.at[q * 2 + e, pl.ds(which * HALF, HALF), :],
                        out.at[pl.ds(core * HALF, HALF), lanes],
                        sems.at[len(copies)],
                    )
                )
                copies[-1].start()
    for copy in copies:
        copy.wait()


def unpack(back):
    return call(
        unpack_kernel,
        "unpack",
        pltpu.HBM((COUNT, 8192), BF16),
        [ANY],
        ANY,
        0,
        4 * 2**20,
        scratch_shapes=[pltpu.SemaphoreType.DMA((32,))],
    )(back)


def peaks_kernel(mine, other, out):
    high = jnp.maximum(mine[:, :, KW:WIDE], other[:, :, KW:WIDE]).astype(F32)
    high = jnp.max(high, axis=0)
    out[...] = jnp.maximum(high[0:8], high[8:16])


def peaks_of(mine, other):
    return call(peaks_kernel, "peaks_of", array((8, 128), F32), [VMEM] * 2, VMEM, 2**15, 2**17)(mine, other)


def last_kernel(a, b, out):
    high = jnp.maximum(a[...], b[...])
    low = lax.broadcasted_iota(jnp.int32, (8, 128), 1) < 64
    out[0] = jnp.max(jnp.where(low, high, 0.0))
    out[1] = jnp.max(jnp.where(low, 0.0, high))


def last(a, b):
    smem = pl.BlockSpec(memory_space=pltpu.SMEM)
    return call(last_kernel, "last", array((2,), F32), [VMEM] * 2, smem, 2**12, 2**13)(a, b)


def merge_kernel(mine, other, out):
    turn = lax.rem(lax.axis_index("core") + lax.axis_index("z"), 2)
    for source, s in ((mine, turn), (other, 1 - turn)):
        for yh in range(4):
            for t in range(4):
                row = pl.multiple_of(t * 128 + s * 64 + yh * 16, 16)
                out[pl.ds(row, 16), :] = source[t % 2 * 8 + yh * 2 + t // 2, :, 0:KW].astype(F32)


def merge(mine, other):
    return call(merge_kernel, "merge", array((512, KW), F32), [VMEM] * 2, VMEM, 0, 2 * 2**20)(mine, other)


def from_ahead(x, axis, size, step):
    return lax.ppermute(x, axis, [((i + step) % size, i) for i in range(size)])


def with_neighbours(peaks, step):
    ahead = from_ahead(peaks, "z", 8, step)
    behind = from_ahead(peaks, "z", 8, 8 - step)
    return jnp.maximum(peaks, jnp.maximum(ahead, behind))


def swap(x):
    return from_ahead(x, "core", 2, 1)


def shift_weight(weight):
    pairs = [(q * 8 + (z + SHIFT[q]) % 8, q * 8 + z) for q in range(8) for z in range(8)]
    return lax.ppermute(weight, ("yl", "xh", "core", "z"), pairs)


def local(tokens, key_grad, weight_codes, block_scales):
    factor = 1.0 / math.sqrt(512 * COUNT)

    packed, weight = pack(tokens, key_grad, weight_codes, block_scales)
    weight = shift_weight(weight)
    got = lax.all_to_all(packed, GROUP, 0, 0, tiled=True)
    got, weight, across = lax.optimization_barrier((got, weight, swap(weight)))
    other = swap(away(got))
    total, mine = home(got)
    share = join(total, other)
    back, high = product(mine, weight, across)

    terms = lax.all_to_all(share, SPREAD, 0, 0, tiled=True)
    piece, peaks = reduce_terms(factor, terms, high)

    plane = lax.all_to_all(spread(piece, peaks), PLANE, 0, 0, tiled=True)

    back, plane = lax.optimization_barrier((back, plane))
    back = lax.all_to_all(back, GROUP, 0, 0, tiled=True)
    other = swap(plane)
    peaks = with_neighbours(peaks_of(plane, other), 1)
    weight_grad = merge(plane, other)
    weight_grad, peaks = lax.optimization_barrier((weight_grad, peaks))
    peaks = with_neighbours(peaks, 3)
    input_grad = unpack(back)
    input_grad, across = lax.optimization_barrier((input_grad, from_ahead(peaks, "xl", 2, 1)))
    return (input_grad, weight_grad, last(peaks, across))


def solution(mesh):
    fine = Mesh(mesh.devices.reshape(SIZES), AXES)
    return jax.shard_map(
        local,
        mesh=fine,
        in_specs=(P(AXES, None), P(AXES, None), P(("z", "xl"), None), P(("z", "xl"))),
        out_specs=(P(AXES, None), P(("z", "xl"), None), P()),
        check_vma=False,
    )
```

```python
import math

import jax
import jax.numpy as jnp
from jax import lax
from jax.experimental import pallas as pl
from jax.experimental.pallas import tpu as pltpu
from jax.sharding import Mesh
from jax.sharding import PartitionSpec as P

QBLOCK = 128
AXES = ("yh", "yl", "xh", "core", "z", "xl")
SIZES = (4, 2, 2, 2, 8, 2)
GROUP = ("xh", "xl", "core", "yl")
SPREAD = ("yh", "z")
PLANE = ("xh", "yh", "yl")
SHIFT = (0, 4, 1, 7, 2, 6, 3, 5)
BF16 = jnp.bfloat16
F32 = jnp.float32
COUNT = 128
HALF = COUNT // 2
KW = 512
PACK = COUNT + HALF
WIDE = KW + 128
PARAMS = pltpu.CompilerParams(vmem_limit_bytes=24 * 2**20)
VMEM = pl.BlockSpec(memory_space=pltpu.VMEM)
ANY = pl.BlockSpec(memory_space=pl.ANY)


def call(kernel, name, out_shape, in_specs, out_specs, flops, moved, **more):
    return pl.pallas_call(
        kernel,
        in_specs=in_specs,
        out_specs=out_specs,
        out_shape=out_shape,
        compiler_params=PARAMS,
        cost_estimate=pl.CostEstimate(flops=flops, bytes_accessed=moved, transcendentals=0),
        name=name,
        **more,
    )


def array(shape, dtype=BF16):
    return jax.ShapeDtypeStruct(shape, dtype)


def pack_kernel(tokens, keys, codes, scales, out, weight, columns, own, held, ready, scaled, factors, sems):
    loads = [
        pltpu.make_async_copy(tokens.at[:, pl.ds(z * 1024, 1024)], columns.at[z], sems.at[z]) for z in range(8)
    ]
    loads.append(pltpu.make_async_copy(keys, own, sems.at[8]))
    loads.append(pltpu.make_async_copy(codes, held, sems.at[9]))
    loads.append(pltpu.make_async_copy(scales, factors, sems.at[15]))
    for load in loads[8:] + loads[:8]:
        load.start()
    stores = []
    loads[9].wait()
    loads[10].wait()
    for block in range(4):
        rows = pl.ds(block * QBLOCK, QBLOCK)
        scaled[rows, :] = (held[rows, :].astype(F32) * factors[block]).astype(BF16)
    stores.append(pltpu.make_async_copy(scaled, weight, sems.at[10]))
    stores[-1].start()
    loads[8].wait()
    for part in range(16):
        core = part // 2 % 2
        ready[part, COUNT:PACK, :] = own[core * HALF : (core + 1) * HALF, :]
    low = lax.broadcasted_iota(jnp.int32, (HALF, 128), 1) < 64
    for m in range(4):
        loads[2 * m].wait()
        loads[2 * m + 1].wait()
        lanes = pl.ds(m * 128, 128)
        for t in range(4):
            for e in range(2):
                for half in range(2):
                    rows = pl.ds(half * HALF, HALF)
                    column = pl.ds(e * 512 + t * 128, 128)
                    even = columns[2 * m, rows, column]
                    odd = columns[2 * m + 1, rows, column]
                    for core in range(2):
                        first, second = (even, odd) if core == 0 else (odd, even)
                        at = HALF * (half ^ core)
                        ready[t % 2 * 8 + e * 4 + half * 2 + t // 2, at : at + HALF, lanes] = jnp.where(low, first, second)
        stores.append(pltpu.make_async_copy(ready.at[:, :, lanes], out.at[:, :, lanes], sems.at[11 + m]))
        stores[-1].start()
    for store in stores:
        store.wait()


def hbm(x):
    return pltpu.with_memory_space_constraint(x, pltpu.HBM)


def pack(tokens, key_grad, codes, scales):
    return call(
        pack_kernel,
        "pack",
        [pltpu.HBM((16, PACK, KW), BF16), pltpu.HBM((512, KW), BF16)],
        [ANY] * 4,
        [ANY] * 2,
        0,
        9 * 2**20,
        scratch_shapes=[
            pltpu.VMEM((8, COUNT, 1024), BF16),
            pltpu.VMEM((COUNT, KW), BF16),
            pltpu.VMEM((512, KW), BF16),
            pltpu.VMEM((16, PACK, KW), BF16),
            pltpu.VMEM((512, KW), BF16),
            pltpu.SMEM((4,), F32),
            pltpu.SemaphoreType.DMA((16,)),
        ],
    )(hbm(tokens), hbm(key_grad), hbm(codes), hbm(scales))


def gradients(rows, keys):
    return lax.dot_general(
        rows.reshape(-1, KW), keys.reshape(-1, KW), (((0,), (0,)), ((), ())), preferred_element_type=F32
    )


def products(keys, weight):
    out = lax.dot_general(
        keys.reshape(-1, KW), weight, (((1,), (1,)), ((), ())), preferred_element_type=F32
    ).astype(BF16)
    return out, jnp.max(jnp.abs(out.astype(F32)).reshape(-1, 8, KW), axis=0)


def away_kernel(got, out):
    out[...] = gradients(got[:, HALF:COUNT, :], got[:, COUNT:PACK, :]).astype(BF16)


def away(got):
    return call(away_kernel, "away", array((KW, KW)), [VMEM], VMEM, 2**29, 3 * 2**20)(got)


def home_kernel(got, total, mine, sem):
    copy = pltpu.make_async_copy(got.at[:, pl.ds(COUNT, HALF), :], mine, sem)
    copy.start()
    total[...] = gradients(got[:, 0:HALF, :], got[:, COUNT:PACK, :])
    copy.wait()


def home(got):
    return call(
        home_kernel,
        "home",
        [array((KW, KW), F32), pltpu.HBM((16, HALF, KW), BF16)],
        [VMEM],
        [VMEM, ANY],
        2**29,
        4 * 2**20,
        scratch_shapes=[pltpu.SemaphoreType.DMA],
    )(got)


def join_kernel(total, other, share, chunks, sem):
    core = lax.axis_index("core")
    summed = (total[...] + other[...].astype(F32)).astype(BF16)
    for m in range(4):
        for s in range(2):
            z = 2 * m + jnp.where(core == 0, s, 1 - s)
            for yh in range(4):
                row = m * 128 + s * 64 + yh * 16
                chunks[yh * 8 + z] = summed[row : row + 16, :]
    store = pltpu.make_async_copy(chunks, share, sem)
    store.start()
    store.wait()


def join(total, other):
    return call(
        join_kernel,
        "join",
        pltpu.HBM((32, 16, KW), BF16),
        [VMEM] * 2,
        ANY,
        2**18,
        2**21,
        scratch_shapes=[pltpu.VMEM((32, 16, KW), BF16), pltpu.SemaphoreType.DMA],
    )(total, other)


def product_kernel(mine, weight, across, back, high, keys, scaled, rest, sems):
    loads = [
        pltpu.make_async_copy(mine, keys, sems.at[0]),
        pltpu.make_async_copy(weight, scaled.at[0], sems.at[1]),
        pltpu.make_async_copy(across, scaled.at[1], sems.at[2]),
    ]
    for load in loads:
        load.start()
    loads[0].wait()
    stores = []
    sizes = []
    for which in range(2):
        loads[1 + which].wait()
        out, size = products(keys[...], scaled[which])
        sizes.append(size)
        rest[which] = out.reshape(16, HALF, KW)
        rows = pl.ds(which * HALF, HALF)
        stores.append(pltpu.make_async_copy(rest.at[which], back.at[:, rows, :], sems.at[3 + which]))
        stores[-1].start()
    high[...] = jnp.maximum(sizes[0], sizes[1])
    for store in stores:
        store.wait()


def product(mine, weight, across):
    return call(
        product_kernel,
        "product",
        [pltpu.HBM((16, COUNT, KW), BF16), array((8, KW), F32)],
        [ANY] * 3,
        [ANY, VMEM],
        2**30,
        5 * 2**20,
        scratch_shapes=[
            pltpu.VMEM((16, HALF, KW), BF16),
            pltpu.VMEM((2, KW, KW), BF16),
            pltpu.VMEM((2, 16, HALF, KW), BF16),
            pltpu.SemaphoreType.DMA((5,)),
        ],
    )(hbm(mine), hbm(weight), hbm(across))


def reduce_kernel(factor, terms, high, piece, peaks):
    total = terms[0].astype(F32)
    for k in range(1, 32):
        total += terms[k].astype(F32)
    rounded = (total * factor).astype(BF16)
    piece[...] = rounded
    first = jnp.max(high[...])
    second = jnp.max(jnp.abs(rounded.astype(F32)))
    lane = lax.broadcasted_iota(jnp.int32, (8, 128), 1)
    peaks[...] = jnp.where(lane < 64, first, second)


def reduce_terms(factor, terms, high):
    return call(
        lambda *refs: reduce_kernel(factor, *refs),
        "reduce_terms",
        [array((16, KW)), array((8, 128), F32)],
        [VMEM] * 2,
        [VMEM] * 2,
        2**18,
        2**20,
    )(terms, high)


def spread_kernel(piece, peaks, out):
    line = jnp.concatenate([peaks[...], peaks[...]], axis=0).astype(BF16)
    for k in range(16):
        out[k, :, 0:KW] = piece[...]
        out[k, :, KW:WIDE] = line


def spread(piece, peaks):
    return call(spread_kernel, "spread", array((16, 16, WIDE)), [VMEM] * 2, VMEM, 0, 2**19)(piece, peaks)


def unpack_kernel(back, out, sems):
    z = lax.axis_index("z")
    copies = []
    for q in range(8):
        core = q % 2
        for which in range(2):
            place = lax.rem(z + SHIFT[q ^ which], 8) * 1024
            for e in range(2):
                lanes = pl.ds(pl.multiple_of(place + e * 512, 512), 512)
                copies.append(
                    pltpu.make_async_copy(
                        back.at[q // 2 % 2 * 8 + e * 4 + core * 2 + q // 4, pl.ds(which * HALF, HALF), :],
                        out.at[pl.ds(core * HALF, HALF), lanes],
                        sems.at[len(copies)],
                    )
                )
                copies[-1].start()
    for copy in copies:
        copy.wait()


def unpack(back):
    return call(
        unpack_kernel,
        "unpack",
        pltpu.HBM((COUNT, 8192), BF16),
        [ANY],
        ANY,
        0,
        4 * 2**20,
        scratch_shapes=[pltpu.SemaphoreType.DMA((32,))],
    )(back)


def peaks_kernel(mine, other, out):
    high = jnp.maximum(mine[:, :, KW:WIDE], other[:, :, KW:WIDE]).astype(F32)
    high = jnp.max(high, axis=0)
    out[...] = jnp.maximum(high[0:8], high[8:16])


def peaks_of(mine, other):
    return call(peaks_kernel, "peaks_of", array((8, 128), F32), [VMEM] * 2, VMEM, 2**15, 2**17)(mine, other)


def last_kernel(a, b, out):
    high = jnp.maximum(a[...], b[...])
    low = lax.broadcasted_iota(jnp.int32, (8, 128), 1) < 64
    out[0] = jnp.max(jnp.where(low, high, 0.0))
    out[1] = jnp.max(jnp.where(low, 0.0, high))


def last(a, b):
    smem = pl.BlockSpec(memory_space=pltpu.SMEM)
    return call(last_kernel, "last", array((2,), F32), [VMEM] * 2, smem, 2**12, 2**13)(a, b)


def merge_kernel(mine, other, out):
    turn = lax.rem(lax.axis_index("core") + lax.axis_index("z"), 2)
    for source, s in ((mine, turn), (other, 1 - turn)):
        for yh in range(4):
            for t in range(4):
                row = pl.multiple_of(t * 128 + s * 64 + yh * 16, 16)
                out[pl.ds(row, 16), :] = source[t % 2 * 8 + yh * 2 + t // 2, :, 0:KW].astype(F32)


def merge(mine, other):
    return call(merge_kernel, "merge", array((512, KW), F32), [VMEM] * 2, VMEM, 0, 2 * 2**20)(mine, other)


def from_ahead(x, axis, size, step):
    return lax.ppermute(x, axis, [((i + step) % size, i) for i in range(size)])


def with_neighbours(peaks, step):
    ahead = from_ahead(peaks, "z", 8, step)
    behind = from_ahead(peaks, "z", 8, 8 - step)
    return jnp.maximum(peaks, jnp.maximum(ahead, behind))


def swap(x):
    return from_ahead(x, "core", 2, 1)


def shift_weight(weight):
    pairs = [(q * 8 + (z + SHIFT[q]) % 8, q * 8 + z) for q in range(8) for z in range(8)]
    return lax.ppermute(weight, ("yl", "xh", "core", "z"), pairs)


def local(tokens, key_grad, weight_codes, block_scales):
    factor = 1.0 / math.sqrt(512 * COUNT)

    packed, weight = pack(tokens, key_grad, weight_codes, block_scales)
    weight = shift_weight(weight)
    got = lax.all_to_all(packed, GROUP, 0, 0, tiled=True)
    got, weight, across = lax.optimization_barrier((got, weight, swap(weight)))
    other = swap(away(got))
    total, mine = home(got)
    share = join(total, other)
    back, high = product(mine, weight, across)

    terms = lax.all_to_all(share, SPREAD, 0, 0, tiled=True)
    piece, peaks = reduce_terms(factor, terms, high)

    plane = lax.all_to_all(spread(piece, peaks), PLANE, 0, 0, tiled=True)

    back, plane = lax.optimization_barrier((back, plane))
    back = lax.all_to_all(back, GROUP, 0, 0, tiled=True)
    other = swap(plane)
    peaks = with_neighbours(peaks_of(plane, other), 1)
    weight_grad = merge(plane, other)
    weight_grad, peaks = lax.optimization_barrier((weight_grad, peaks))
    peaks = with_neighbours(peaks, 3)
    input_grad = unpack(back)
    input_grad, across = lax.optimization_barrier((input_grad, from_ahead(peaks, "xl", 2, 1)))
    return (input_grad, weight_grad, last(peaks, across))


def solution(mesh):
    fine = Mesh(mesh.devices.reshape(SIZES), AXES)
    return jax.shard_map(
        local,
        mesh=fine,
        in_specs=(P(AXES, None), P(AXES, None), P(("z", "xl"), None), P(("z", "xl"))),
        out_specs=(P(AXES, None), P(("z", "xl"), None), P()),
        check_vma=False,
    )
```

```python
import math

import jax
import jax.numpy as jnp
from jax import lax
from jax.experimental import pallas as pl
from jax.experimental.pallas import tpu as pltpu
from jax.sharding import Mesh
from jax.sharding import PartitionSpec as P

QBLOCK = 128
AXES = ("yh", "yl", "xh", "core", "z", "xl")
SIZES = (4, 2, 2, 2, 8, 2)
GROUP = ("xh", "xl", "core", "yl")
SPREAD = ("z", "yh")
PLANE = ("xh", "yh", "yl")
SHIFT = (0, 4, 1, 7, 2, 6, 3, 5)
BF16 = jnp.bfloat16
F32 = jnp.float32
COUNT = 128
HALF = COUNT // 2
KW = 512
PACK = COUNT + HALF
WIDE = KW + 128
PARAMS = pltpu.CompilerParams(vmem_limit_bytes=24 * 2**20)
VMEM = pl.BlockSpec(memory_space=pltpu.VMEM)
ANY = pl.BlockSpec(memory_space=pl.ANY)


def call(kernel, name, out_shape, in_specs, out_specs, flops, moved, **more):
    return pl.pallas_call(
        kernel,
        in_specs=in_specs,
        out_specs=out_specs,
        out_shape=out_shape,
        compiler_params=PARAMS,
        cost_estimate=pl.CostEstimate(flops=flops, bytes_accessed=moved, transcendentals=0),
        name=name,
        **more,
    )


def array(shape, dtype=BF16):
    return jax.ShapeDtypeStruct(shape, dtype)


def pack_kernel(tokens, keys, codes, scales, out, weight, columns, own, held, ready, scaled, factors, sems):
    loads = [
        pltpu.make_async_copy(tokens.at[:, pl.ds(z * 1024, 1024)], columns.at[z], sems.at[z]) for z in range(8)
    ]
    loads.append(pltpu.make_async_copy(keys, own, sems.at[8]))
    loads.append(pltpu.make_async_copy(codes, held, sems.at[9]))
    loads.append(pltpu.make_async_copy(scales, factors, sems.at[15]))
    for load in loads[8:] + loads[:8]:
        load.start()
    stores = []
    loads[9].wait()
    loads[10].wait()
    for block in range(4):
        rows = pl.ds(block * QBLOCK, QBLOCK)
        scaled[rows, :] = (held[rows, :].astype(F32) * factors[block]).astype(BF16)
    stores.append(pltpu.make_async_copy(scaled, weight, sems.at[10]))
    stores[-1].start()
    loads[8].wait()
    for part in range(16):
        core = part // 2 % 2
        ready[part, COUNT:PACK, :] = own[core * HALF : (core + 1) * HALF, :]
    low = lax.broadcasted_iota(jnp.int32, (HALF, 128), 1) < 64
    for m in range(4):
        loads[2 * m].wait()
        loads[2 * m + 1].wait()
        lanes = pl.ds(m * 128, 128)
        for t in range(4):
            for e in range(2):
                for half in range(2):
                    rows = pl.ds(half * HALF, HALF)
                    column = pl.ds(e * 512 + t * 128, 128)
                    even = columns[2 * m, rows, column]
                    odd = columns[2 * m + 1, rows, column]
                    for core in range(2):
                        first, second = (even, odd) if core == 0 else (odd, even)
                        at = HALF * (half ^ core)
                        ready[t % 2 * 8 + e * 4 + half * 2 + t // 2, at : at + HALF, lanes] = jnp.where(low, first, second)
        stores.append(pltpu.make_async_copy(ready.at[:, :, lanes], out.at[:, :, lanes], sems.at[11 + m]))
        stores[-1].start()
    for store in stores:
        store.wait()


def hbm(x):
    return pltpu.with_memory_space_constraint(x, pltpu.HBM)


def pack(tokens, key_grad, codes, scales):
    return call(
        pack_kernel,
        "pack",
        [pltpu.HBM((16, PACK, KW), BF16), pltpu.HBM((512, KW), BF16)],
        [ANY] * 4,
        [ANY] * 2,
        0,
        9 * 2**20,
        scratch_shapes=[
            pltpu.VMEM((8, COUNT, 1024), BF16),
            pltpu.VMEM((COUNT, KW), BF16),
            pltpu.VMEM((512, KW), BF16),
            pltpu.VMEM((16, PACK, KW), BF16),
            pltpu.VMEM((512, KW), BF16),
            pltpu.SMEM((4,), F32),
            pltpu.SemaphoreType.DMA((16,)),
        ],
    )(hbm(tokens), hbm(key_grad), hbm(codes), hbm(scales))


def gradients(rows, keys):
    return lax.dot_general(
        rows.reshape(-1, KW), keys.reshape(-1, KW), (((0,), (0,)), ((), ())), preferred_element_type=F32
    )


def products(keys, weight):
    out = lax.dot_general(
        keys.reshape(-1, KW), weight, (((1,), (1,)), ((), ())), preferred_element_type=F32
    ).astype(BF16)
    return out, jnp.max(jnp.abs(out.astype(F32)).reshape(-1, 8, KW), axis=0)


def away_kernel(got, out):
    out[...] = gradients(got[:, HALF:COUNT, :], got[:, COUNT:PACK, :]).astype(BF16)


def away(got):
    return call(away_kernel, "away", array((KW, KW)), [VMEM], VMEM, 2**29, 3 * 2**20)(got)


def home_kernel(got, total, mine, sem):
    copy = pltpu.make_async_copy(got.at[:, pl.ds(COUNT, HALF), :], mine, sem)
    copy.start()
    total[...] = gradients(got[:, 0:HALF, :], got[:, COUNT:PACK, :])
    copy.wait()


def home(got):
    return call(
        home_kernel,
        "home",
        [array((KW, KW), F32), pltpu.HBM((16, HALF, KW), BF16)],
        [VMEM],
        [VMEM, ANY],
        2**29,
        4 * 2**20,
        scratch_shapes=[pltpu.SemaphoreType.DMA],
    )(got)


def join_kernel(total, other, share, chunks, sem):
    core = lax.axis_index("core")
    summed = (total[...] + other[...].astype(F32)).astype(BF16)
    for m in range(4):
        for s in range(2):
            z = 2 * m + jnp.where(core == 0, s, 1 - s)
            for yh in range(4):
                row = m * 128 + s * 64 + yh * 16
                chunks[z * 4 + yh] = summed[row : row + 16, :]
    store = pltpu.make_async_copy(chunks, share, sem)
    store.start()
    store.wait()


def join(total, other):
    return call(
        join_kernel,
        "join",
        pltpu.HBM((32, 16, KW), BF16),
        [VMEM] * 2,
        ANY,
        2**18,
        2**21,
        scratch_shapes=[pltpu.VMEM((32, 16, KW), BF16), pltpu.SemaphoreType.DMA],
    )(total, other)


def product_kernel(mine, weight, across, back, high, keys, scaled, rest, sems):
    loads = [
        pltpu.make_async_copy(mine, keys, sems.at[0]),
        pltpu.make_async_copy(weight, scaled.at[0], sems.at[1]),
        pltpu.make_async_copy(across, scaled.at[1], sems.at[2]),
    ]
    for load in loads:
        load.start()
    loads[0].wait()
    stores = []
    sizes = []
    for which in range(2):
        loads[1 + which].wait()
        out, size = products(keys[...], scaled[which])
        sizes.append(size)
        rest[which] = out.reshape(16, HALF, KW)
        rows = pl.ds(which * HALF, HALF)
        stores.append(pltpu.make_async_copy(rest.at[which], back.at[:, rows, :], sems.at[3 + which]))
        stores[-1].start()
    high[...] = jnp.maximum(sizes[0], sizes[1])
    for store in stores:
        store.wait()


def product(mine, weight, across):
    return call(
        product_kernel,
        "product",
        [pltpu.HBM((16, COUNT, KW), BF16), array((8, KW), F32)],
        [ANY] * 3,
        [ANY, VMEM],
        2**30,
        5 * 2**20,
        scratch_shapes=[
            pltpu.VMEM((16, HALF, KW), BF16),
            pltpu.VMEM((2, KW, KW), BF16),
            pltpu.VMEM((2, 16, HALF, KW), BF16),
            pltpu.SemaphoreType.DMA((5,)),
        ],
    )(hbm(mine), hbm(weight), hbm(across))


def reduce_kernel(factor, terms, high, piece, peaks):
    total = terms[0].astype(F32)
    for k in range(1, 32):
        total += terms[k].astype(F32)
    rounded = (total * factor).astype(BF16)
    piece[...] = rounded
    first = jnp.max(high[...])
    second = jnp.max(jnp.abs(rounded.astype(F32)))
    lane = lax.broadcasted_iota(jnp.int32, (8, 128), 1)
    peaks[...] = jnp.where(lane < 64, first, second)


def reduce_terms(factor, terms, high):
    return call(
        lambda *refs: reduce_kernel(factor, *refs),
        "reduce_terms",
        [array((16, KW)), array((8, 128), F32)],
        [VMEM] * 2,
        [VMEM] * 2,
        2**18,
        2**20,
    )(terms, high)


def spread_kernel(piece, peaks, out):
    line = jnp.concatenate([peaks[...], peaks[...]], axis=0).astype(BF16)
    for k in range(16):
        out[k, :, 0:KW] = piece[...]
        out[k, :, KW:WIDE] = line


def spread(piece, peaks):
    return call(spread_kernel, "spread", array((16, 16, WIDE)), [VMEM] * 2, VMEM, 0, 2**19)(piece, peaks)


def unpack_kernel(back, out, sems):
    z = lax.axis_index("z")
    copies = []
    for q in range(8):
        core = q % 2
        for which in range(2):
            place = lax.rem(z + SHIFT[q ^ which], 8) * 1024
            for e in range(2):
                lanes = pl.ds(pl.multiple_of(place + e * 512, 512), 512)
                copies.append(
                    pltpu.make_async_copy(
                        back.at[q // 2 % 2 * 8 + e * 4 + core * 2 + q // 4, pl.ds(which * HALF, HALF), :],
                        out.at[pl.ds(core * HALF, HALF), lanes],
                        sems.at[len(copies)],
                    )
                )
                copies[-1].start()
    for copy in copies:
        copy.wait()


def unpack(back):
    return call(
        unpack_kernel,
        "unpack",
        pltpu.HBM((COUNT, 8192), BF16),
        [ANY],
        ANY,
        0,
        4 * 2**20,
        scratch_shapes=[pltpu.SemaphoreType.DMA((32,))],
    )(back)


def peaks_kernel(mine, other, out):
    high = jnp.maximum(mine[:, :, KW:WIDE], other[:, :, KW:WIDE]).astype(F32)
    high = jnp.max(high, axis=0)
    out[...] = jnp.maximum(high[0:8], high[8:16])


def peaks_of(mine, other):
    return call(peaks_kernel, "peaks_of", array((8, 128), F32), [VMEM] * 2, VMEM, 2**15, 2**17)(mine, other)


def last_kernel(a, b, out):
    high = jnp.maximum(a[...], b[...])
    low = lax.broadcasted_iota(jnp.int32, (8, 128), 1) < 64
    out[0] = jnp.max(jnp.where(low, high, 0.0))
    out[1] = jnp.max(jnp.where(low, 0.0, high))


def last(a, b):
    smem = pl.BlockSpec(memory_space=pltpu.SMEM)
    return call(last_kernel, "last", array((2,), F32), [VMEM] * 2, smem, 2**12, 2**13)(a, b)


def merge_kernel(mine, other, out):
    turn = lax.rem(lax.axis_index("core") + lax.axis_index("z"), 2)
    for source, s in ((mine, turn), (other, 1 - turn)):
        for yh in range(4):
            for t in range(4):
                row = pl.multiple_of(t * 128 + s * 64 + yh * 16, 16)
                out[pl.ds(row, 16), :] = source[t % 2 * 8 + yh * 2 + t // 2, :, 0:KW].astype(F32)


def merge(mine, other):
    return call(merge_kernel, "merge", array((512, KW), F32), [VMEM] * 2, VMEM, 0, 2 * 2**20)(mine, other)


def from_ahead(x, axis, size, step):
    return lax.ppermute(x, axis, [((i + step) % size, i) for i in range(size)])


def with_neighbours(peaks, step):
    ahead = from_ahead(peaks, "z", 8, step)
    behind = from_ahead(peaks, "z", 8, 8 - step)
    return jnp.maximum(peaks, jnp.maximum(ahead, behind))


def swap(x):
    return from_ahead(x, "core", 2, 1)


def shift_weight(weight):
    pairs = [(q * 8 + (z + SHIFT[q]) % 8, q * 8 + z) for q in range(8) for z in range(8)]
    return lax.ppermute(weight, ("yl", "xh", "core", "z"), pairs)


def local(tokens, key_grad, weight_codes, block_scales):
    factor = 1.0 / math.sqrt(512 * COUNT)

    packed, weight = pack(tokens, key_grad, weight_codes, block_scales)
    weight = shift_weight(weight)
    got = lax.all_to_all(packed, GROUP, 0, 0, tiled=True)
    got, weight, across = lax.optimization_barrier((got, weight, swap(weight)))
    other = swap(away(got))
    total, mine = home(got)
    share = join(total, other)
    back, high = product(mine, weight, across)

    terms = lax.all_to_all(share, SPREAD, 0, 0, tiled=True)
    piece, peaks = reduce_terms(factor, terms, high)

    plane = lax.all_to_all(spread(piece, peaks), PLANE, 0, 0, tiled=True)

    back, plane = lax.optimization_barrier((back, plane))
    back = lax.all_to_all(back, GROUP, 0, 0, tiled=True)
    other = swap(plane)
    peaks = with_neighbours(peaks_of(plane, other), 1)
    weight_grad = merge(plane, other)
    weight_grad, peaks = lax.optimization_barrier((weight_grad, peaks))
    peaks = with_neighbours(peaks, 3)
    input_grad = unpack(back)
    input_grad, across = lax.optimization_barrier((input_grad, from_ahead(peaks, "xl", 2, 1)))
    return (input_grad, weight_grad, last(peaks, across))


def solution(mesh):
    fine = Mesh(mesh.devices.reshape(SIZES), AXES)
    return jax.shard_map(
        local,
        mesh=fine,
        in_specs=(P(AXES, None), P(AXES, None), P(("z", "xl"), None), P(("z", "xl"))),
        out_specs=(P(AXES, None), P(("z", "xl"), None), P()),
        check_vma=False,
    )
```
